256 devices in a mesh: tm: 8 (over y, x_lo), space: 32 (over z, x_hi, core).
Axes of the slice: x: 4 (x_hi: 2, x_lo: 2; x = x_hi * 2 + x_lo), y: 4, z: 8, core: 2. Of those that a mesh axis runs over, the one named last changes fastest.
Arguments:
- video: bfloat16 [16, 256, 128, 128], P('tm', 'space'), may hold values from -6 to 6
- norm_gain: float32 [128], replicated, may hold values from 0.25 to 1.75
- conv_weight: bfloat16 [3, 3, 3, 128, 128], replicated, may hold values from -0.109375 to 0.109375
- conv_bias: float32 [128], replicated, may hold values from -1.5 to 1.5
- down_weight: bfloat16 [3, 3, 3, 128, 256], replicated, may hold values from -0.109375 to 0.109375
- down_bias: float32 [256], replicated, may hold values from -1.5 to 1.5
- attention_gain: float32 [256], replicated, may hold values from 0.25 to 1.75
- query_weight: bfloat16 [256, 256], replicated, may hold values from -4 to 4
- key_weight: bfloat16 [256, 256], replicated, may hold values from -0.375 to 0.375
- value_weight: bfloat16 [256, 256], replicated, may hold values from -0.375 to 0.375
- output_weight: bfloat16 [256, 256], replicated, may hold values from -0.375 to 0.375
Outputs:
- encoded: float32 [16, 128, 64, 256], P('tm', 'space')
The draws below stay inside these ranges and needn't reach their ends.
All inputs are finite; a program needn't handle non-finite values.
Results may differ from the reference program's by a relative error of at most 0.02.
The reference program's roundings to bfloat16 on the way (of `activated`, `summed`, `normed`, `weights` and `attended`) count: a program that leaves them out, or rounds other values in their place, can miss the bound.
Values may be sent and summed in bfloat16 or wider, within the bound.
No kernel may reach another device: no remote copies, remote signals or barrier semaphores. Data moves between devices by JAX's collectives and lax.ppermute only.
A program may use at most 128 MiB of HBM per device.

```python
import math
import jax
import jax.numpy as jnp
from jax import lax

C1 = 128
C2 = 256
COLS = 128
FRAMES = 16
ROWS = 256


def draw_query_weight(key, part):
    key = jax.random.fold_in(key, 1)
    base = jax.random.normal(key, (C2, C2), jnp.float32)
    scaled = base * (1.0 / math.sqrt(C2))
    return jnp.clip(scaled, -4.0, 4.0).astype(jnp.bfloat16)


def level_of(stream_key, dims, cuts, least, high):
    gain = 1.0
    for dim, shards_of in cuts:
        steps = jax.random.uniform(jax.random.fold_in(jax.random.fold_in(stream_key, 6), dim), (shards_of,), jnp.float32, least / len(cuts), high / len(cuts))
        gain = gain * jnp.repeat(jnp.exp(steps), dims[dim] // shards_of).reshape((-1,) + (1,) * (len(dims) - 1 - dim))
    return gain


def bell_draw(rng, shape, width, most, pieces=(), held_as=jnp.bfloat16):
    array = jax.random.normal(rng, shape, jnp.float32) * width
    if len(pieces) > 0:
        array = level_of(rng, shape, pieces, -0.22, 0.18) * array
    return jnp.clip(array, min=-most, max=most).astype(held_as)


def setup_inputs(seed: int = 0) -> dict:
    streams_of = jax.random.split(jax.random.key(seed), 12)
    return {
        "video": bell_draw(streams_of[0], (FRAMES, ROWS, COLS, C1), 1.0, 6.0, ((0, 8), (1, 32))),
        "norm_gain": jnp.clip(1.0 + 0.15 * jax.random.normal(streams_of[1], (C1,), jnp.float32), 0.25, 1.75),
        "conv_weight": bell_draw(streams_of[2], (3, 3, 3, C1, C1), (27 * C1) ** -0.5, 0.109375),
        "conv_bias": bell_draw(streams_of[3], (C1,), 0.3, 1.5, (), jnp.float32),
        "down_weight": bell_draw(streams_of[4], (3, 3, 3, C1, C2), (27 * C1) ** -0.5, 0.109375),
        "down_bias": bell_draw(streams_of[5], (C2,), 0.3, 1.5, (), jnp.float32),
        "attention_gain": jnp.clip(1.0 + 0.15 * jax.random.normal(streams_of[6], (C2,), jnp.float32), 0.25, 1.75),
        "query_weight": draw_query_weight(jax.random.fold_in(streams_of[11], 71), 0),
        "key_weight": bell_draw(streams_of[8], (C2, C2), C2 ** -0.5, 0.375),
        "value_weight": bell_draw(streams_of[9], (C2, C2), C2 ** -0.5, 0.375),
        "output_weight": bell_draw(streams_of[10], (C2, C2), C2 ** -0.5, 0.375),
    }


epsilon = 1e-05

def layer_norm(inputs, gain_vec):
    values_f = inputs.astype(jnp.float32)
    average = lax.optimization_barrier(jnp.mean(values_f, axis=-1, keepdims=True))
    spread = lax.optimization_barrier(jnp.mean((values_f - average) ** 2, axis=-1, keepdims=True))
    return (values_f - average) * lax.rsqrt(spread + epsilon) * gain_vec

def convolve(inputs, kernel, strides):
    result = lax.conv_general_dilated(inputs[None], kernel, strides, 'VALID', dimension_numbers=('NDHWC', 'DHWIO', 'NDHWC'), preferred_element_type=jnp.float32)
    return result[0]

def attend_frame(operands):
    queries, keys, values = operands
    scores = jnp.dot(queries, keys.T, preferred_element_type=jnp.float32) * queries.shape[-1] ** (-0.5)
    highest = lax.optimization_barrier(jnp.max(scores, axis=-1, keepdims=True))
    weights = jnp.exp(scores - highest).astype(jnp.bfloat16)
    totals = lax.optimization_barrier(jnp.sum(weights.astype(jnp.float32), axis=-1, keepdims=True))
    return (jnp.dot(weights, values, preferred_element_type=jnp.float32) / totals).astype(jnp.bfloat16)

def reference(video, norm_gain, conv_weight, conv_bias, down_weight, down_bias, attention_gain, query_weight, key_weight, value_weight, output_weight):
    activated = jax.nn.silu(layer_norm(video, norm_gain)).astype(jnp.bfloat16)
    padded = jnp.pad(activated, ((2, 0), (1, 1), (1, 1), (0, 0)))
    summed = (video.astype(jnp.float32) + convolve(padded, conv_weight, (1, 1, 1)) + conv_bias).astype(jnp.bfloat16)
    widened = jnp.pad(summed, ((2, 0), (0, 1), (0, 1), (0, 0)))
    reduced = convolve(widened, down_weight, (1, 2, 2)) + down_bias
    normed = layer_norm(reduced, attention_gain).astype(jnp.bfloat16)
    frame_count, row_count, col_count, channels = reduced.shape
    flattened = normed.reshape(-1, channels)
    queries = jnp.dot(flattened, query_weight, preferred_element_type=jnp.float32).astype(jnp.bfloat16)
    keys = jnp.dot(flattened, key_weight, preferred_element_type=jnp.float32).astype(jnp.bfloat16)
    values = jnp.dot(flattened, value_weight, preferred_element_type=jnp.float32).astype(jnp.bfloat16)
    shape_frames = (frame_count, row_count * col_count, channels)
    attended = lax.map(attend_frame, (queries.reshape(shape_frames), keys.reshape(shape_frames), values.reshape(shape_frames)))
    mixed = jnp.dot(attended.reshape(-1, channels), output_weight, preferred_element_type=jnp.float32)
    encoded = reduced + mixed.reshape(reduced.shape)
    return encoded.astype(jnp.float32)
```

```python
import jax
import jax.numpy as jnp
from jax import lax
from jax.experimental import pallas as pl
from jax.experimental.pallas import tpu as pltpu
from jax.sharding import PartitionSpec as P

epsilon = 1e-05
f32 = jnp.float32
bf16 = jnp.bfloat16
VMEM = pl.BlockSpec(memory_space=pltpu.VMEM)
SMEM = pl.BlockSpec(memory_space=pltpu.SMEM)
COLS = 128
C1 = 128
C2 = 256
ROWS = 8
HALF = 64
QUERIES = 256


def call(kernel, outs, ins, scratch=(), scalars=0, aliases=None, flops=0, nbytes=0):
    return pl.pallas_call(
        kernel,
        out_shape=[jax.ShapeDtypeStruct(s, d) for s, d in outs],
        in_specs=[SMEM] * scalars + [VMEM] * (len(ins) - scalars),
        out_specs=[VMEM] * len(outs),
        scratch_shapes=list(scratch),
        input_output_aliases=aliases or {},
        compiler_params=pltpu.CompilerParams(vmem_limit_bytes=48 * 1024 * 1024),
        cost_estimate=pl.CostEstimate(flops=flops, bytes_accessed=nbytes, transcendentals=0),
    )(*ins)


def dot(a, b):
    return jnp.dot(a, b, preferred_element_type=f32)


def averaging():
    i = lax.broadcasted_iota(jnp.int32, (2 * C1, 2 * C1), 0) // C1
    j = lax.broadcasted_iota(jnp.int32, (2 * C1, 2 * C1), 1) // C1
    return jnp.where(i == j, 1.0 / C1, 0.0).astype(bf16)


def activate(pair, gain2, mean_of):
    centred = pair.astype(f32) - dot(pair, mean_of)
    squares = centred * centred
    high = squares.astype(bf16)
    low = (squares - high.astype(f32)).astype(bf16)
    spread = dot(high, mean_of) + dot(low, mean_of)
    y = centred * lax.rsqrt(spread + epsilon) * gain2
    return y / (1.0 + jnp.exp(-y))


def store_shifted(taps, row, act):
    col = lax.broadcasted_iota(jnp.int32, act.shape, 0)
    at = pl.ds(row * COLS, COLS)
    taps[0, at, :] = jnp.where(col == 0, 0.0, pltpu.roll(act, 1, 0)).astype(bf16)
    taps[1, at, :] = act.astype(bf16)
    taps[2, at, :] = jnp.where(col == COLS - 1, 0.0, pltpu.roll(act, COLS - 1, 0)).astype(bf16)


def fill_taps(taps, above, middle, below, gain_ref):
    gain2 = jnp.concatenate([gain_ref[...], gain_ref[...]], axis=1)
    mean_of = averaging()

    def put(row, ref, i):
        pair = jnp.concatenate([ref[0, i], ref[1, i]], axis=1)
        store_shifted(taps, row, activate(pair, gain2, mean_of))

    for row in range(ROWS + 3):
        if row < 1:
            put(row, above[0], above[1])
        elif row <= ROWS:
            put(row, middle, row - 1)
        else:
            put(row, below[0], below[1] + row - ROWS - 1)


def conv1_taps(taps, acc, weight_of, first):
    size = (ROWS + 1) * COLS
    for kr in range(3):
        for kc in range(3):
            part = dot(taps[kc, kr * COLS : kr * COLS + size, :], weight_of(kr, kc))
            if first and kr == 0 and kc == 0:
                acc[...] = part
            else:
                acc[...] += part


def stack(a, b, c, d):
    return jnp.concatenate([jnp.concatenate([a, b], axis=1), jnp.concatenate([c, d], axis=1)], axis=0)


def own_kernel(video, above, below, gain, weight, acc, taps):
    fill_taps(taps, (above, 0), video, (below, 0), gain)
    none = jnp.zeros((C1, C1), bf16)

    def weight_of(kr, kc):
        return stack(weight[2, kr, kc], weight[1, kr, kc], none, weight[2, kr, kc])

    conv1_taps(taps, acc, weight_of, True)


def halo_kernel(
    last, acc_in, halo, corner, video, below, gain, weight, bias, down, send, half_taps, acc, taps, wide
):
    fill_taps(taps, (corner, 0), halo, (corner, 1), gain)
    none = jnp.zeros((C1, C1), bf16)

    def weight_of(kr, kc):
        return stack(weight[0, kr, kc], none, weight[1, kr, kc], weight[0, kr, kc])

    acc[...] = acc_in[...]
    conv1_taps(taps, acc, weight_of, False)
    bias2 = jnp.concatenate([bias[...], bias[...]], axis=1)
    keep = jnp.where(last[0] == 1, 0.0, 1.0)
    for row in range(ROWS + 1):
        src, i = (video, row) if row < ROWS else (below, 0)
        pair = jnp.concatenate([src[0, i], src[1, i]], axis=1).astype(f32)
        at = pl.ds(row * COLS, COLS)
        summed = (pair + acc[at, :] + bias2).astype(bf16).astype(f32)
        if row == ROWS:
            summed = summed * keep
        wide[0, at, :] = summed[:, :C1]
        wide[1, at, :] = summed[:, C1:]
    j = lax.broadcasted_iota(jnp.int32, (HALF, C1), 0)
    for row in range(ROWS + 1):
        place = row // 2 if row % 2 == 0 else 5 + row // 2
        for frame in range(2):
            even = wide[frame, pl.ds(row * COLS, HALF, stride=2), :]
            odd = wide[frame, pl.ds(row * COLS + 1, HALF, stride=2), :]
            after = jnp.where(j == HALF - 1, 0.0, pltpu.roll(even, HALF - 1, 0))
            lanes = pl.ds(frame * C1, C1)
            at = pl.ds(place * HALF, HALF)
            half_taps[0, at, lanes] = even.astype(bf16)
            half_taps[1, at, lanes] = odd.astype(bf16)
            half_taps[2, at, lanes] = after.astype(bf16)
    first = jnp.zeros((QUERIES, C2), f32)
    second = jnp.zeros((QUERIES, C2), f32)
    for kr in range(3):
        start = (0, 5 * HALF, HALF)[kr]
        for kc in range(3):
            tile = half_taps[kc, start : start + QUERIES, :]
            first += dot(tile, jnp.concatenate([down[0, kr, kc], down[1, kr, kc]], axis=0))
            second += dot(tile[:, C1:], down[0, kr, kc])
    send[0] = first.astype(bf16)
    send[1] = second.astype(bf16)


def down_kernel(half_taps, down, bias, out):
    first = jnp.zeros((QUERIES, C2), f32) + bias[...]
    second = jnp.zeros((QUERIES, C2), f32) + bias[...]
    for kr in range(3):
        start = (0, 5 * HALF, HALF)[kr]
        for kc in range(3):
            tile = half_taps[kc, start : start + QUERIES, :]
            first += dot(tile[:, :C1], down[2, kr, kc])
            second += dot(tile, jnp.concatenate([down[1, kr, kc], down[2, kr, kc]], axis=0))
    out[0] = first
    out[1] = second


def norm_kernel(mine, part, received, gain, reduced, keep, send):
    frames = []
    for frame in range(2):
        value = part[frame] + received[frame].astype(f32)
        reduced[frame] = value
        centred = value - jnp.mean(value, axis=1, keepdims=True)
        spread = jnp.mean(centred * centred, axis=1, keepdims=True)
        frames.append(centred * lax.rsqrt(spread + epsilon) * gain[...])
    pick = mine[0] == 0
    keep[...] = jnp.where(pick, frames[0], frames[1]).astype(bf16)
    send[...] = jnp.where(pick, frames[1], frames[0]).astype(bf16)


TILE = 256
BLOCK = 2 * QUERIES
ALL = 2 * BLOCK


def attend_block(queries, total, top, mass, block, key_weight, value_weight, first):
    normed = block[...]
    keys = dot(normed, key_weight[...]).astype(bf16)
    values = dot(normed, value_weight[...]).astype(bf16)
    for tile in range(ALL // TILE):
        at = pl.ds(tile * TILE, TILE)
        scores = lax.dot_general(
            queries[at, :], keys, (((1,), (1,)), ((), ())), preferred_element_type=f32
        )
        highest = jnp.max(scores, axis=1, keepdims=True)
        if not first:
            old = top[at, :]
            new = jnp.maximum(old, highest)
            rescale = jnp.exp(old - new)
            highest = new[:, :1]
        else:
            new = jnp.broadcast_to(highest, (TILE, 128))
        weights = jnp.exp(scores - highest).astype(bf16)
        gathered = weights.astype(f32)
        sums = sum(gathered[:, i * 128 : (i + 1) * 128] for i in range(BLOCK // 128))
        product = dot(weights, values)
        if first:
            mass[at, :] = sums
            total[at, :] = product
        else:
            mass[at, :] = mass[at, :] * rescale + sums
            total[at, :] = total[at, :] * rescale[:, :1] + product
        top[at, :] = new


def first_attend_kernel(own, other, query_weight, key_weight, value_weight, queries, total, top, mass):
    scale = C2**-0.5
    for i, ref in enumerate((own, other)):
        at = pl.ds(i * BLOCK, BLOCK)
        queries[at, :] = (dot(ref[...], query_weight[...]).astype(bf16) * scale).astype(bf16)
    attend_block(queries, total, top, mass, own, key_weight, value_weight, True)


def attend_kernel(count, last, *refs):
    queries, total_in, top_in, mass_in = refs[:4]
    blocks = refs[4 : 4 + count]
    key_weight, value_weight = refs[4 + count : 6 + count]
    if last:
        mine, theirs, total, top, mass = refs[6 + count :]
    else:
        total, top, mass = refs[6 + count :]
    total[...] = total_in[...]
    top[...] = top_in[...]
    mass[...] = mass_in[...]
    for block in blocks:
        attend_block(queries, total, top, mass, block, key_weight, value_weight, False)
    if last:
        for out, at in ((mine, pl.ds(0, BLOCK)), (theirs, pl.ds(BLOCK, BLOCK))):
            out[:, :C2] = total[at, :]
            out[:, C2 : C2 + 128] = top[at, :]
            whole = jnp.sum(mass[at, :], axis=1, keepdims=True)
            out[:, C2 + 128 :] = jnp.broadcast_to(whole, (BLOCK, 128))


def merge_kernel(mine, theirs, keep, send):
    top_a, top_b = mine[:, C2 : C2 + 128], theirs[:, C2 : C2 + 128]
    top = jnp.maximum(top_a, top_b)
    scale_a, scale_b = jnp.exp(top_a - top), jnp.exp(top_b - top)
    inverse = 1.0 / (mine[:, C2 + 128 :] * scale_a + theirs[:, C2 + 128 :] * scale_b)
    scale_a, scale_b = scale_a * inverse, scale_b * inverse
    attended = (mine[:, :C2] * scale_a[:, :1] + theirs[:, :C2] * scale_b[:, :1]).astype(bf16)
    keep[...] = attended[:QUERIES]
    send[...] = attended[QUERIES:]


def last_kernel(mine, reduced, keep, received, weight, out):
    here = mine[0]
    there = 1 - here
    out[here] = reduced[here] + dot(keep[...], weight[...])
    out[there] = reduced[there] + dot(received[...], weight[...])


def body(
    video,
    norm_gain,
    conv_weight,
    conv_bias,
    down_weight,
    down_bias,
    attention_gain,
    query_weight,
    key_weight,
    value_weight,
    output_weight,
):
    space = lax.axis_size("space")
    times = lax.axis_size("tm")
    place = lax.axis_index("space")
    is_last = (place == space - 1).astype(jnp.int32).reshape(1)
    frame = ((place // 2) % 2).astype(jnp.int32).reshape(1)
    gain = norm_gain.reshape(1, C1)

    def next_frames(x):
        return lax.ppermute(x, "tm", [(i, i + 1) for i in range(times - 1)])

    def along_z(x, distance):
        return lax.ppermute(x, "space", [(i, (i + 4 * distance) % space) for i in range(space)])

    def swap(x, bit):
        return lax.ppermute(x, "space", [(i, i ^ bit) for i in range(space)])

    above = lax.ppermute(video[:, -1:], "space", [(i, i + 1) for i in range(space - 1)])
    below = lax.ppermute(video[:, :2], "space", [(i + 1, i) for i in range(space - 1)])
    halo = next_frames(video)
    corner = next_frames(jnp.concatenate([above, below], axis=1))

    size = (ROWS + 1) * COLS
    taps = pltpu.VMEM((3, (ROWS + 3) * COLS, 2 * C1), bf16)
    (acc,) = call(
        own_kernel,
        [((size, 2 * C1), f32)],
        [video, above, below, gain, conv_weight],
        [taps],
        flops=2 * 9 * size * 256 * 256,
        nbytes=3_000_000,
    )
    send, half_taps = call(
        halo_kernel,
        [((2, QUERIES, C2), bf16), ((3, 9 * HALF, 2 * C1), bf16)],
        [is_last, acc, halo, corner, video, below, gain, conv_weight, conv_bias.reshape(1, C1), down_weight],
        [pltpu.VMEM((size, 2 * C1), f32), taps, pltpu.VMEM((2, size, C1), f32)],
        scalars=1,
        flops=2 * 9 * size * 256 * 256 + 2 * 18 * 256 * 256 * 256,
        nbytes=6_000_000,
    )
    received = next_frames(send)
    (part,) = call(
        down_kernel,
        [((2, QUERIES, C2), f32)],
        [half_taps, down_weight, down_bias.reshape(1, C2)],
        flops=2 * 18 * 256 * 256 * 256,
        nbytes=3_000_000,
    )
    reduced, keep, give = call(
        norm_kernel,
        [((2, QUERIES, C2), f32), ((QUERIES, C2), bf16), ((QUERIES, C2), bf16)],
        [frame, part, received, attention_gain.reshape(1, C2)],
        scalars=1,
        nbytes=2_000_000,
    )
    own = jnp.concatenate([keep, swap(give, 2)], axis=0)
    plus, minus = along_z(own, 1), along_z(own, -1)
    other = swap(own, 1)
    state = [((ALL, C2), f32), ((ALL, 128), f32), ((ALL, 128), f32)]
    block_flops = 2 * BLOCK * 256 * (512 + 2 * ALL)
    queries, *carry = call(
        first_attend_kernel,
        [((ALL, C2), bf16)] + state,
        [own, other, query_weight, key_weight, value_weight],
        flops=block_flops,
        nbytes=4_000_000,
    )
    for step in range(1, 4):
        blocks = [plus, minus]
        plus = along_z(plus, 1)
        if step < 3:
            minus = along_z(minus, -1)
        carry = call(
            lambda *refs: attend_kernel(2, False, *refs),
            state,
            [queries, *carry, *blocks, key_weight, value_weight],
            aliases={1: 0, 2: 1, 3: 2},
            flops=2 * block_flops,
            nbytes=6_000_000,
        )
    ends = [((BLOCK, C2 + 256), f32)] * 2
    mine, theirs = call(
        lambda *refs: attend_kernel(1, True, *refs),
        ends,
        [queries, *carry, plus, key_weight, value_weight],
        [pltpu.VMEM(s, d) for s, d in state],
        flops=block_flops,
        nbytes=6_000_000,
    )
    theirs = swap(theirs, 1)
    keep, give = call(
        merge_kernel,
        [((QUERIES, C2), bf16)] * 2,
        [mine, theirs],
        nbytes=3_000_000,
    )
    back = swap(give, 2)
    (encoded,) = call(
        last_kernel,
        [((2, QUERIES, C2), f32)],
        [frame, reduced, keep, back, output_weight],
        scalars=1,
        nbytes=2_000_000,
    )
    return encoded.reshape(2, ROWS // 2, HALF, C2)


def solution(mesh):
    in_specs = (P("tm", "space", None, None), P(), P(), P(), P(), P(), P(), P(), P(), P(), P())
    out_specs = P("tm", "space", None, None)
    return jax.shard_map(body, mesh=mesh, in_specs=in_specs, out_specs=out_specs, check_vma=False)
```

```python
import jax
import jax.numpy as jnp
from jax import lax
from jax.experimental import pallas as pl
from jax.experimental.pallas import tpu as pltpu
from jax.sharding import PartitionSpec as P

epsilon = 1e-05
f32 = jnp.float32
bf16 = jnp.bfloat16
VMEM = pl.BlockSpec(memory_space=pltpu.VMEM)
SMEM = pl.BlockSpec(memory_space=pltpu.SMEM)
HBM = pl.BlockSpec(memory_space=pltpu.HBM)
COLS = 128
C1 = 128
C2 = 256
ROWS = 8
HALF = 64
QUERIES = 256


def call(kernel, outs, ins, scratch=(), spaces=None, aliases=None, flops=0, nbytes=0):
    spaces = spaces or {}
    ins = [
        pltpu.with_memory_space_constraint(x, pltpu.HBM) if spaces.get(i) is HBM else x
        for i, x in enumerate(ins)
    ]
    return pl.pallas_call(
        kernel,
        out_shape=[jax.ShapeDtypeStruct(s, d) for s, d in outs],
        in_specs=[spaces.get(i, VMEM) for i in range(len(ins))],
        out_specs=[VMEM] * len(outs),
        scratch_shapes=list(scratch),
        input_output_aliases=aliases or {},
        compiler_params=pltpu.CompilerParams(vmem_limit_bytes=24 * 1024 * 1024),
        cost_estimate=pl.CostEstimate(flops=flops, bytes_accessed=nbytes, transcendentals=0),
    )(*ins)


def dot(a, b):
    return jnp.dot(a, b, preferred_element_type=f32)


def dot_t(a, b):
    return lax.dot_general(a, b, (((1,), (1,)), ((), ())), preferred_element_type=f32)


def averaging():
    i = lax.broadcasted_iota(jnp.int32, (2 * C1, 2 * C1), 0) // C1
    j = lax.broadcasted_iota(jnp.int32, (2 * C1, 2 * C1), 1) // C1
    return jnp.where(i == j, 1.0 / C1, 0.0).astype(bf16)


def activate(pair, gain2, mean_of):
    centred = pair.astype(f32) - dot(pair, mean_of)
    squares = centred * centred
    high = squares.astype(bf16)
    low = (squares - high.astype(f32)).astype(bf16)
    spread = dot(high, mean_of) + dot(low, mean_of)
    y = centred * lax.rsqrt(spread + epsilon) * gain2
    return y / (1.0 + jnp.exp(-y))


def store_shifted(taps, row, act):
    col = lax.broadcasted_iota(jnp.int32, act.shape, 0)
    at = pl.ds(row * COLS, COLS)
    taps[0, at, :] = jnp.where(col == 0, 0.0, pltpu.roll(act, 1, 0)).astype(bf16)
    taps[1, at, :] = act.astype(bf16)
    taps[2, at, :] = jnp.where(col == COLS - 1, 0.0, pltpu.roll(act, COLS - 1, 0)).astype(bf16)


def pair_of(ref, i):
    return jnp.concatenate([ref[0, i], ref[1, i]], axis=1)


def fill_taps(taps, rows, gain_ref):
    gain2 = jnp.concatenate([gain_ref[...], gain_ref[...]], axis=1)
    mean_of = averaging()
    for row, ref, i, factor in rows:
        act = activate(pair_of(ref, i), gain2, mean_of)
        store_shifted(taps, row, act if factor is None else act * factor)


SIZE = (ROWS + 1) * COLS


def conv1_taps(taps, weight, acc, base):
    for kr in range(3):
        tile = jnp.concatenate([taps[kc, kr * COLS : kr * COLS + SIZE, :] for kc in range(3)], axis=1)
        part = dot(tile, weight[kr].reshape(3 * C2, C2))
        acc[...] = (acc[...] if kr else base()) + part


def stack(a, b, c, d):
    return jnp.concatenate([jnp.concatenate([a, b], axis=1), jnp.concatenate([c, d], axis=1)], axis=0)


def edge_kernel(video, bottom, top, sem):
    copies = [
        pltpu.make_async_copy(video.at[:, ROWS - 1 : ROWS], bottom, sem.at[0]),
        pltpu.make_async_copy(video.at[:, 0:2], top, sem.at[1]),
    ]
    for copy in copies:
        copy.start()
    for copy in copies:
        copy.wait()


def blank_edges(taps):
    for row in (0, ROWS + 1, ROWS + 2):
        taps[:, row * COLS : (row + 1) * COLS, :] = jnp.zeros((3, COLS, C2), bf16)


def own_kernel(
    video_h, gain_h, bias_h, conv_h, down_h, query_h, key_h, value_h, output_h, down_bias_h, attention_gain_h,
    acc, now, before, down, query, key, value_t, output, gain, down_bias, attention_gain,
    taps, video, bias, conv, value, sem,
):
    pairs = (
        (gain_h, gain), (video_h, video), (bias_h, bias), (conv_h, conv), (value_h, value), (down_h, down),
        (query_h, query), (key_h, key), (output_h, output),
        (down_bias_h, down_bias), (attention_gain_h, attention_gain),
    )
    copies = [pltpu.make_async_copy(src, dst, sem.at[i]) for i, (src, dst) in enumerate(pairs)]
    for copy in copies:
        copy.start()
    blank_edges(taps)
    for copy in copies[:3]:
        copy.wait()
    fill_taps(taps, [(row + 1, video, row, None) for row in range(ROWS)], gain)
    copies[3].wait()
    none = jnp.zeros((C1, C1), bf16)
    for kr in range(3):
        for kc in range(3):
            w0, w1, w2 = (conv[kt, kr, kc] for kt in range(3))
            now[kr, kc] = stack(w2, w1, none, w2)
            before[kr, kc] = stack(w0, none, w1, w0)

    def base():
        bias2 = jnp.concatenate([bias[...], bias[...]], axis=1)
        rows = [pair_of(video, i).astype(f32) for i in range(ROWS)] + [jnp.zeros((COLS, C2), f32)]
        return jnp.concatenate(rows, axis=0) + bias2

    conv1_taps(taps, now, acc, base)
    copies[4].wait()
    value_t[...] = value[...].astype(f32).T.astype(bf16)
    for copy in copies[5:]:
        copy.wait()


def halo_kernel(flags, acc_in, halo, gain, weight, acc, taps):
    blank_edges(taps)
    fill_taps(taps, [(row + 1, halo, row, flags[0]) for row in range(ROWS)], gain)
    conv1_taps(taps, weight, acc, lambda: acc_in[...])


def sum_kernel(
    flags, acc_in, above, below, far_above, far_below, gain, now, before, down,
    send, half_taps, acc, taps, far_taps, wide,
):
    past = flags[0]
    edges = [(0, above, 0, flags[1]), (1, below, 0, flags[2]), (2, below, 1, flags[2])]
    fill_taps(taps, edges, gain)
    edges = [(0, far_above, 0, flags[1]), (1, far_below, 0, flags[2]), (2, far_below, 1, flags[2])]
    fill_taps(far_taps, [(row, ref, i, factor * past) for row, ref, i, factor in edges], gain)

    def add(kr, taps_row, count, row):
        tile = jnp.concatenate(
            [
                source[kc, taps_row * COLS : (taps_row + count) * COLS, :]
                for source in (taps, far_taps)
                for kc in range(3)
            ],
            axis=1,
        )
        weight = jnp.concatenate([now[kr].reshape(3 * C2, C2), before[kr].reshape(3 * C2, C2)], axis=0)
        at = pl.ds(row * COLS, count * COLS)
        acc[at, :] += dot(tile, weight)

    acc[...] = acc_in[...]
    acc[pl.ds(ROWS * COLS, COLS), :] += pair_of(below, 0).astype(f32)
    add(0, 0, 1, 0)
    add(1, 1, 1, ROWS)
    add(2, 1, 2, ROWS - 1)
    for row in range(ROWS + 1):
        at = pl.ds(row * COLS, COLS)
        summed = acc[at, :].astype(bf16).astype(f32)
        if row == ROWS:
            summed = summed * flags[2]
        wide[0, at, :] = summed[:, :C1]
        wide[1, at, :] = summed[:, C1:]
    j = lax.broadcasted_iota(jnp.int32, (HALF, C1), 0)
    for row in range(ROWS + 1):
        place = row // 2 if row % 2 == 0 else 5 + row // 2
        for frame in range(2):
            even = wide[frame, pl.ds(row * COLS, HALF, stride=2), :]
            odd = wide[frame, pl.ds(row * COLS + 1, HALF, stride=2), :]
            after = jnp.where(j == HALF - 1, 0.0, pltpu.roll(even, HALF - 1, 0))
            lanes = pl.ds(frame * C1, C1)
            at = pl.ds(place * HALF, HALF)
            half_taps[0, at, lanes] = even.astype(bf16)
            half_taps[1, at, lanes] = odd.astype(bf16)
            half_taps[2, at, lanes] = after.astype(bf16)
    first = jnp.zeros((QUERIES, C2), f32)
    second = jnp.zeros((QUERIES, C2), f32)
    for kr in range(3):
        start = (0, 5 * HALF, HALF)[kr]
        for kc in range(3):
            tile = half_taps[kc, start : start + QUERIES, :]
            first += dot(tile, jnp.concatenate([down[0, kr, kc], down[1, kr, kc]], axis=0))
            second += dot(tile[:, C1:], down[0, kr, kc])
    send[0] = first.astype(bf16)
    send[1] = second.astype(bf16)


def down_kernel(half_taps, down, bias, out):
    first = jnp.zeros((QUERIES, C2), f32) + bias[...]
    second = jnp.zeros((QUERIES, C2), f32) + bias[...]
    for kr in range(3):
        start = (0, 5 * HALF, HALF)[kr]
        for kc in range(3):
            tile = half_taps[kc, start : start + QUERIES, :]
            first += dot(tile[:, :C1], down[2, kr, kc])
            second += dot(tile, jnp.concatenate([down[1, kr, kc], down[2, kr, kc]], axis=0))
    out[0] = first
    out[1] = second


def norm_kernel(flags, part, received, gain, reduced, normed):
    for frame in range(2):
        value = part[frame] + received[frame].astype(f32) * flags[0]
        reduced[frame] = value
        centred = value - jnp.mean(value, axis=1, keepdims=True)
        spread = jnp.mean(centred * centred, axis=1, keepdims=True)
        normed[frame] = (centred * lax.rsqrt(spread + epsilon) * gain[...]).astype(bf16)


GROUPS = 4
STATE = C2 + 16


def attend(queries, before, outs, blocks, key_weight, value_weight_t, groups=range(4)):
    normed = jnp.concatenate([block[...] for block in blocks], axis=0)
    keys = dot(normed, key_weight[...]).astype(bf16)
    values = dot_t(value_weight_t[...], normed).astype(bf16)
    values = jnp.concatenate([values, jnp.ones((16, values.shape[1]), bf16)], axis=0)
    ahead = dot_t(keys, queries[groups[0]])
    for i, group in enumerate(groups):
        scores = ahead
        if i + 1 < len(groups):
            ahead = dot_t(keys, queries[groups[i + 1]])
        highest = jnp.max(scores, axis=0, keepdims=True)
        if before is not None:
            old = before[group, C2 + 8 : C2 + 9, :]
            highest = jnp.maximum(old, highest)
            rescale = jnp.exp(old - highest)
        weights = jnp.exp(scores - highest).astype(bf16)
        product = dot(values, weights)[: C2 + 8]
        if before is not None:
            product += before[group, : C2 + 8, :] * rescale
        out, place = outs(group)
        out[place, : C2 + 8, :] = product
        out[place, C2 + 8 :, :] = jnp.broadcast_to(highest, (8, C2))


def query_kernel(normed, weight, queries):
    for frame in range(2):
        queries[frame] = (dot(normed[frame], weight[...]).astype(bf16) * (C2**-0.5)).astype(bf16)


def first_attend_kernel(
    frame, own, sibling, across, both, block, plus, minus, key_weight, value_weight_t, queries, state
):
    for group, source in enumerate((own, sibling, across, both)):
        queries[group] = source[frame]
    blocks = [ref.at[frame] for ref in (block, plus, minus)]
    attend(queries, None, lambda g: (state, g), blocks, key_weight, value_weight_t)


def attend_kernel(frame, queries, before, plus, minus, key_weight, value_weight_t, state):
    blocks = [ref.at[frame] for ref in (plus, minus)]
    attend(queries, before, lambda g: (state, g), blocks, key_weight, value_weight_t)


def cut_kernel(plus, minus, first, second):
    first[...] = plus[0]
    second[...] = minus[1]


def last_attend_kernel(groups, *refs):
    queries, before, blocks = refs[0:2], refs[2:4], refs[4:6]
    key_weight, value_weight_t, mine, theirs = refs[6:]
    for frame in range(2):
        attend(
            queries[frame],
            before[frame],
            lambda g: (mine if g == groups[0] else theirs, frame),
            (blocks[frame],),
            key_weight,
            value_weight_t,
            groups,
        )


def split3(x):
    high = x.astype(bf16).astype(f32)
    middle = (x - high).astype(bf16).astype(f32)
    return [high, middle, x - high - middle]


def merged(mine, theirs, frame):
    top_a, top_b = mine[frame, C2 + 8 :, :], theirs[frame, C2 + 8 :, :]
    top = jnp.maximum(top_a, top_b)
    scale_a, scale_b = jnp.exp(top_a - top), jnp.exp(top_b - top)
    mass = mine[frame, C2 : C2 + 8, :] * scale_a + theirs[frame, C2 : C2 + 8, :] * scale_b
    return mass, top, scale_a, scale_b


def merge_keep_kernel(mine, theirs, state):
    for frame in range(2):
        mass, top, scale_a, scale_b = merged(mine, theirs, frame)
        state[frame, :C2, :] = mine[frame, :C2, :] * scale_a[:1] + theirs[frame, :C2, :] * scale_b[:1]
        state[frame, C2 : C2 + 8, :] = mass
        state[frame, C2 + 8 :, :] = top


def merge_send_kernel(mine, theirs, send):
    for frame in range(2):
        mass, top, scale_a, scale_b = merged(mine, theirs, frame)
        inverse = 1.0 / mass
        scale_a, scale_b = scale_a * inverse, scale_b * inverse
        total = mine[frame, :C2, :] * scale_a[:1] + theirs[frame, :C2, :] * scale_b[:1]
        send[frame, :C2, :] = total.astype(bf16)
        rows = split3(top[:1]) + split3(mass[:1]) + [jnp.zeros((10, C2), f32)]
        send[frame, C2:, :] = jnp.concatenate(rows, axis=0).astype(bf16)


def last_kernel(reduced, state, received, weight, out):
    for frame in range(2):
        rows = received[frame, C2:, :].astype(f32)
        top_a, mass_a = state[frame, C2 + 8 : C2 + 9, :], state[frame, C2 : C2 + 1, :]
        top_b = rows[0:1] + rows[1:2] + rows[2:3]
        mass_b = rows[3:4] + rows[4:5] + rows[5:6]
        top = jnp.maximum(top_a, top_b)
        scale_a = jnp.exp(top_a - top)
        scale_b = jnp.exp(top_b - top) * mass_b
        inverse = 1.0 / (mass_a * scale_a + scale_b)
        attended = state[frame, :C2, :] * (scale_a * inverse)
        attended += received[frame, :C2, :].astype(f32) * (scale_b * inverse)
        mixed = lax.dot_general(
            attended.astype(bf16), weight[...], (((0,), (0,)), ((), ())), preferred_element_type=f32
        )
        out[frame] = reduced[frame] + mixed


def body(
    video,
    norm_gain,
    conv_weight,
    conv_bias,
    down_weight,
    down_bias,
    attention_gain,
    query_weight,
    key_weight,
    value_weight,
    output_weight,
):
    space = lax.axis_size("space")
    times = lax.axis_size("tm")
    place = lax.axis_index("space")
    has = [lax.axis_index("tm") > 0, place > 0, place < space - 1]
    flags = jnp.stack(has).astype(f32)
    scalar = {0: SMEM}

    def next_frames(x):
        return lax.ppermute(x, "tm", [(i, (i + 1) % times) for i in range(times)])

    def along(x, distance):
        return lax.ppermute(x, "space", [(i, (i + distance) % space) for i in range(space)])

    def diagonal(x, distance):
        route = [
            (t * space + i, ((t + 1) % times) * space + (i + distance) % space)
            for t in range(times)
            for i in range(space)
        ]
        return lax.ppermute(x, ("tm", "space"), route)

    def swap(x, bit):
        return lax.ppermute(x, "space", [(i, i ^ bit) for i in range(space)])

    bottom, top = call(
        edge_kernel,
        [((2, 1, COLS, C1), bf16), ((2, 2, COLS, C1), bf16)],
        [video],
        [pltpu.SemaphoreType.DMA((2,))],
        {0: HBM},
        nbytes=400_000,
    )
    above = along(bottom, 1)
    below = along(top, -1)
    halo = next_frames(video)
    far_above, far_below = diagonal(bottom, 1), diagonal(top, -1)

    square = (C2, C2)
    taps = pltpu.VMEM((3, (ROWS + 3) * COLS, C2), bf16)
    whole = ((SIZE, C2), f32)
    prepared = (3, 3) + square
    (
        acc, now, before, down_weight, query_weight, key_weight, value_weight, output_weight,
        gain, down_bias, attention_gain,
    ) = call(
        own_kernel,
        [whole, (prepared, bf16), (prepared, bf16), (down_weight.shape, bf16)]
        + [(square, bf16)] * 4
        + [((1, C1), f32), ((1, C2), f32), ((1, C2), f32)],
        [video, norm_gain.reshape(1, C1), conv_bias.reshape(1, C1), conv_weight, down_weight]
        + [query_weight, key_weight, value_weight, output_weight]
        + [down_bias.reshape(1, C2), attention_gain.reshape(1, C2)],
        [
            taps,
            pltpu.VMEM(video.shape, bf16),
            pltpu.VMEM((1, C1), f32),
            pltpu.VMEM(conv_weight.shape, bf16),
            pltpu.VMEM(square, bf16),
            pltpu.SemaphoreType.DMA((11,)),
        ],
        {i: HBM for i in range(11)},
        flops=2 * 9 * SIZE * 256 * 256,
        nbytes=6_000_000,
    )
    (acc,) = call(
        halo_kernel,
        [whole],
        [flags, acc, halo, gain, before],
        [taps],
        scalar,
        flops=2 * 9 * SIZE * 256 * 256,
        nbytes=5_000_000,
    )
    send, half_taps = call(
        sum_kernel,
        [((2, QUERIES, C2), bf16), ((3, 9 * HALF, C2), bf16)],
        [flags, acc, above, below, far_above, far_below, gain, now, before, down_weight],
        [pltpu.VMEM(*whole)] + [pltpu.VMEM((3, 3 * COLS, C2), bf16)] * 2 + [pltpu.VMEM((2, SIZE, C1), f32)],
        scalar,
        flops=2 * 18 * 256 * 256 * 256,
        nbytes=5_000_000,
    )
    received = next_frames(send)
    (part,) = call(
        down_kernel,
        [((2, QUERIES, C2), f32)],
        [half_taps, down_weight, down_bias],
        flops=2 * 18 * 256 * 256 * 256,
        nbytes=3_000_000,
    )
    pixels = ((2, QUERIES, C2), bf16)
    reduced, normed = call(
        norm_kernel,
        [((2, QUERIES, C2), f32), pixels],
        [flags, part, received, attention_gain],
        spaces=scalar,
        nbytes=2_000_000,
    )
    plus, minus = [along(normed, 4)], [along(normed, -4)]
    (own,) = call(query_kernel, [pixels], [normed, query_weight], nbytes=600_000)
    for step in range(2):
        plus.append(along(plus[step], 4))
        minus.append(along(minus[step], -4))
    given, _ = lax.optimization_barrier((own, plus[0]))
    sibling, across = swap(given, 1), swap(given, 2)
    both = swap(across, 1)
    state = [((GROUPS, STATE, C2), f32)]
    flops = 2 * QUERIES * 256 * (512 + 2 * GROUPS * QUERIES)
    carry, queries = [0, 0], [0, 0]
    weights = [key_weight, value_weight]
    for frame in range(2):
        queries[frame], carry[frame] = call(
            lambda *refs: first_attend_kernel(frame, *refs),
            [((GROUPS, QUERIES, C2), bf16)] + state,
            [own, sibling, across, both, normed, plus[0], minus[0]] + weights,
            flops=3 * flops,
            nbytes=4_000_000,
        )
    (plus[2], minus[2]), carry = lax.optimization_barrier(((plus[2], minus[2]), carry))
    ends = call(cut_kernel, [((QUERIES, C2), bf16)] * 2, [plus[2], minus[2]], nbytes=500_000)
    ends = [along(ends[0], 4), along(ends[1], -4)]
    for step in range(1, 3):
        for frame in range(2):
            (carry[frame],) = call(
                lambda *refs: attend_kernel(frame, *refs),
                state,
                [queries[frame], carry[frame], plus[step], minus[step]] + weights,
                aliases={1: 0},
                flops=2 * flops,
                nbytes=4_000_000,
            )
    pair = ((2, STATE, C2), f32)

    def finish(groups):
        mine, theirs = call(
            lambda *refs: last_attend_kernel(groups, *refs),
            [pair, pair],
            [*queries, *carry, *ends] + weights,
            flops=flops,
            nbytes=4_000_000,
        )
        return mine, swap(theirs, 1)

    (give,) = call(
        merge_send_kernel, [((2, STATE, C2), bf16)], list(finish((2, 3))), nbytes=1_500_000
    )
    received = swap(give, 2)
    (kept,) = call(merge_keep_kernel, [pair], list(finish((0, 1))), nbytes=2_000_000)
    (encoded,) = call(
        last_kernel,
        [((2, QUERIES, C2), f32)],
        [reduced, kept, received, output_weight],
        nbytes=2_000_000,
    )
    return encoded.reshape(2, ROWS // 2, HALF, C2)


def solution(mesh):
    in_specs = (P("tm", "space", None, None), P(), P(), P(), P(), P(), P(), P(), P(), P(), P())
    out_specs = P("tm", "space", None, None)
    return jax.shard_map(body, mesh=mesh, in_specs=in_specs, out_specs=out_specs, check_vma=False)
```

```python
import jax
import jax.numpy as jnp
from jax import lax
from jax.experimental import pallas as pl
from jax.experimental.pallas import tpu as pltpu
from jax.sharding import PartitionSpec as P

epsilon = 1e-05
f32 = jnp.float32
bf16 = jnp.bfloat16
VMEM = pl.BlockSpec(memory_space=pltpu.VMEM)
SMEM = pl.BlockSpec(memory_space=pltpu.SMEM)
HBM = pl.BlockSpec(memory_space=pltpu.HBM)
COLS = 128
C1 = 128
C2 = 256
ROWS = 8
HALF = 64
QUERIES = 256


def call(kernel, outs, ins, scratch=(), spaces=None, aliases=None, flops=0, nbytes=0):
    spaces = spaces or {}
    ins = [
        pltpu.with_memory_space_constraint(x, pltpu.HBM) if spaces.get(i) is HBM else x
        for i, x in enumerate(ins)
    ]
    return pl.pallas_call(
        kernel,
        out_shape=[jax.ShapeDtypeStruct(s, d) for s, d in outs],
        in_specs=[spaces.get(i, VMEM) for i in range(len(ins))],
        out_specs=[VMEM] * len(outs),
        scratch_shapes=list(scratch),
        input_output_aliases=aliases or {},
        compiler_params=pltpu.CompilerParams(vmem_limit_bytes=24 * 1024 * 1024),
        cost_estimate=pl.CostEstimate(flops=flops, bytes_accessed=nbytes, transcendentals=0),
    )(*ins)


def dot(a, b):
    return jnp.dot(a, b, preferred_element_type=f32)


def dot_t(a, b):
    return lax.dot_general(a, b, (((1,), (1,)), ((), ())), preferred_element_type=f32)


def averaging():
    i = lax.broadcasted_iota(jnp.int32, (2 * C1, 2 * C1), 0) // C1
    j = lax.broadcasted_iota(jnp.int32, (2 * C1, 2 * C1), 1) // C1
    return jnp.where(i == j, 1.0 / C1, 0.0).astype(bf16)


def activate(pair, gain2, mean_of):
    centred = pair.astype(f32) - dot(pair, mean_of)
    squares = centred * centred
    high = squares.astype(bf16)
    low = (squares - high.astype(f32)).astype(bf16)
    spread = dot(high, mean_of) + dot(low, mean_of)
    y = centred * lax.rsqrt(spread + epsilon) * gain2
    return y / (1.0 + jnp.exp(-y))


def store_shifted(taps, row, act):
    col = lax.broadcasted_iota(jnp.int32, act.shape, 0)
    at = pl.ds(row * COLS, COLS)
    taps[0, at, :] = jnp.where(col == 0, 0.0, pltpu.roll(act, 1, 0)).astype(bf16)
    taps[1, at, :] = act.astype(bf16)
    taps[2, at, :] = jnp.where(col == COLS - 1, 0.0, pltpu.roll(act, COLS - 1, 0)).astype(bf16)


def pair_of(ref, i):
    return jnp.concatenate([ref[0, i], ref[1, i]], axis=1)


def fill_taps(taps, rows, gain_ref, batch):
    gain2 = jnp.concatenate([gain_ref[...], gain_ref[...]], axis=1)
    mean_of = averaging()
    for start in range(0, len(rows), batch):
        some = rows[start : start + batch]
        pairs = jnp.concatenate([pair_of(ref, i) for _, ref, i, _ in some], axis=0)
        acts = activate(pairs, gain2, mean_of)
        for place, (row, _, _, factor) in enumerate(some):
            act = acts[place * COLS : (place + 1) * COLS]
            store_shifted(taps, row, act if factor is None else act * factor)


SIZE = (ROWS + 1) * COLS


def conv1_taps(taps, weight, acc, base):
    for kr in range(3):
        tile = jnp.concatenate([taps[kc, kr * COLS : kr * COLS + SIZE, :] for kc in range(3)], axis=1)
        part = dot(tile, weight[kr].reshape(3 * C2, C2))
        acc[...] = (acc[...] if kr else base()) + part


def stack(a, b, c, d):
    return jnp.concatenate([jnp.concatenate([a, b], axis=1), jnp.concatenate([c, d], axis=1)], axis=0)


def edge_kernel(video, bottom, top, sem):
    copies = [
        pltpu.make_async_copy(video.at[:, ROWS - 1 : ROWS], bottom, sem.at[0]),
        pltpu.make_async_copy(video.at[:, 0:2], top, sem.at[1]),
    ]
    for copy in copies:
        copy.start()
    for copy in copies:
        copy.wait()


def blank_edges(taps):
    for row in (0, ROWS + 1, ROWS + 2):
        taps[:, row * COLS : (row + 1) * COLS, :] = jnp.zeros((3, COLS, C2), bf16)


def own_kernel(
    video_h, gain_h, bias_h, conv_h, down_h, query_h, key_h, value_h, output_h, down_bias_h, attention_gain_h,
    acc, now, before, down, query, key, value_t, output, gain, down_bias, attention_gain,
    taps, video, bias, conv, value, sem,
):
    pairs = (
        (gain_h, gain), (video_h, video), (bias_h, bias), (conv_h, conv), (value_h, value), (down_h, down),
        (query_h, query), (key_h, key), (output_h, output),
        (down_bias_h, down_bias), (attention_gain_h, attention_gain),
    )
    copies = [pltpu.make_async_copy(src, dst, sem.at[i]) for i, (src, dst) in enumerate(pairs)]
    for copy in copies:
        copy.start()
    blank_edges(taps)
    for copy in copies[:3]:
        copy.wait()
    fill_taps(taps, [(row + 1, video, row, None) for row in range(ROWS)], gain, 4)
    copies[3].wait()
    none = jnp.zeros((C1, C1), bf16)
    for kr in range(3):
        for kc in range(3):
            w0, w1, w2 = (conv[kt, kr, kc] for kt in range(3))
            now[kr, kc] = stack(w2, w1, none, w2)
            before[kr, kc] = stack(w0, none, w1, w0)

    def base():
        bias2 = jnp.concatenate([bias[...], bias[...]], axis=1)
        rows = [pair_of(video, i).astype(f32) for i in range(ROWS)] + [jnp.zeros((COLS, C2), f32)]
        return jnp.concatenate(rows, axis=0) + bias2

    conv1_taps(taps, now, acc, base)
    copies[4].wait()
    value_t[...] = value[...].astype(f32).T.astype(bf16)
    for copy in copies[5:]:
        copy.wait()


def halo_kernel(flags, acc_in, halo, gain, weight, acc, taps):
    blank_edges(taps)
    fill_taps(taps, [(row + 1, halo, row, flags[0]) for row in range(ROWS)], gain, 4)
    conv1_taps(taps, weight, acc, lambda: acc_in[...])


TAPS = [(kr, kc) for kr in range(3) for kc in range(3)]


def down_taps(half_taps, lanes):
    starts = (0, 5 * HALF, HALF)
    tiles = [half_taps[kc, starts[kr] : starts[kr] + QUERIES, lanes] for kr, kc in TAPS]
    return jnp.concatenate(tiles, axis=1)


def down_weights(down, times):
    return jnp.concatenate([down[kt, kr, kc] for kr, kc in TAPS for kt in times], axis=0)


def sum_kernel(
    flags, acc, above, below, far_above, far_below, gain, now, before, down,
    send, half_taps, taps, wide,
):
    past = flags[0]
    edges = [(0, above, 0, flags[1]), (1, below, 0, flags[2]), (2, below, 1, flags[2])]
    far = [(3, far_above, 0, flags[1]), (4, far_below, 0, flags[2]), (5, far_below, 1, flags[2])]
    fill_taps(taps, edges + [(row, ref, i, factor * past) for row, ref, i, factor in far], gain, 3)

    def extra(kr, row, count):
        tile = jnp.concatenate(
            [
                taps[kc, (base + row) * COLS : (base + row + count) * COLS, :]
                for base in (0, 3)
                for kc in range(3)
            ],
            axis=1,
        )
        weight = jnp.concatenate([now[kr].reshape(3 * C2, C2), before[kr].reshape(3 * C2, C2)], axis=0)
        return dot(tile, weight)

    last = extra(2, 1, 2)
    extras = {0: extra(0, 0, 1), ROWS - 1: last[:COLS]}
    extras[ROWS] = last[COLS:] + extra(1, 1, 1) + pair_of(below, 0).astype(f32)
    for row in range(ROWS + 1):
        at = pl.ds(row * COLS, COLS)
        summed = acc[at, :] + extras[row] if row in extras else acc[at, :]
        summed = summed.astype(bf16).astype(f32)
        if row == ROWS:
            summed = summed * flags[2]
        wide[0, at, :] = summed[:, :C1]
        wide[1, at, :] = summed[:, C1:]
    j = lax.broadcasted_iota(jnp.int32, (HALF, C1), 0)
    for row in range(ROWS + 1):
        place = row // 2 if row % 2 == 0 else 5 + row // 2
        for frame in range(2):
            even = wide[frame, pl.ds(row * COLS, HALF, stride=2), :]
            odd = wide[frame, pl.ds(row * COLS + 1, HALF, stride=2), :]
            after = jnp.where(j == HALF - 1, 0.0, pltpu.roll(even, HALF - 1, 0))
            lanes = pl.ds(frame * C1, C1)
            at = pl.ds(place * HALF, HALF)
            half_taps[0, at, lanes] = even.astype(bf16)
            half_taps[1, at, lanes] = odd.astype(bf16)
            half_taps[2, at, lanes] = after.astype(bf16)
    send[0] = dot(down_taps(half_taps, slice(None)), down_weights(down, (0, 1))).astype(bf16)
    send[1] = dot(down_taps(half_taps, slice(C1, None)), down_weights(down, (0,))).astype(bf16)


def down_kernel(half_taps, down, bias, out):
    out[0] = dot(down_taps(half_taps, slice(0, C1)), down_weights(down, (2,))) + bias[...]
    out[1] = dot(down_taps(half_taps, slice(None)), down_weights(down, (1, 2))) + bias[...]


def norm_kernel(flags, part, received, gain, query_weight, reduced, normed, queries):
    value = part[...] + received[...].astype(f32) * flags[0]
    reduced[...] = value
    centred = value - jnp.mean(value, axis=2, keepdims=True)
    spread = jnp.mean(centred * centred, axis=2, keepdims=True)
    result = (centred * lax.rsqrt(spread + epsilon) * gain[...]).astype(bf16)
    normed[...] = result
    for frame in range(2):
        queries[frame] = (dot(result[frame], query_weight[...]).astype(bf16) * (C2**-0.5)).astype(bf16)


GROUPS = 4
STATE = C2 + 16


def attend(queries, before, outs, blocks, key_weight, value_weight_t, groups=range(4)):
    normed = jnp.concatenate([block[...] for block in blocks], axis=0)
    keys = dot(normed, key_weight[...]).astype(bf16)
    values = dot_t(value_weight_t[...], normed).astype(bf16)
    values = jnp.concatenate([values, jnp.ones((16, values.shape[1]), bf16)], axis=0)
    ahead = dot_t(keys, queries[groups[0]])
    for i, group in enumerate(groups):
        scores = ahead
        if i + 1 < len(groups):
            ahead = dot_t(keys, queries[groups[i + 1]])
        highest = jnp.max(scores, axis=0, keepdims=True)
        if before is not None:
            old = before[group, C2 + 8 : C2 + 9, :]
            highest = jnp.maximum(old, highest)
            rescale = jnp.exp(old - highest)
        weights = jnp.exp(scores - highest).astype(bf16)
        product = dot(values, weights)[: C2 + 8]
        if before is not None:
            product += before[group, : C2 + 8, :] * rescale
        out, place = outs(group)
        out[place, : C2 + 8, :] = product
        out[place, C2 + 8 :, :] = jnp.broadcast_to(highest, (8, C2))


def first_attend_kernel(
    frame, own, sibling, across, both, block, plus, minus, key_weight, value_weight_t, queries, state
):
    for group, source in enumerate((own, sibling, across, both)):
        queries[group] = source[frame]
    blocks = [ref.at[frame] for ref in (block, plus, minus)]
    attend(queries, None, lambda g: (state, g), blocks, key_weight, value_weight_t)


def attend_kernel(frame, queries, before, plus, minus, key_weight, value_weight_t, state):
    blocks = [ref.at[frame] for ref in (plus, minus)]
    attend(queries, before, lambda g: (state, g), blocks, key_weight, value_weight_t)


def cut_kernel(plus, minus, first, second):
    first[...] = plus[0]
    second[...] = minus[1]


def last_attend_kernel(groups, *refs):
    queries, before, blocks = refs[0:2], refs[2:4], refs[4:6]
    key_weight, value_weight_t, mine, theirs = refs[6:]
    for frame in range(2):
        attend(
            queries[frame],
            before[frame],
            lambda g: (mine if g == groups[0] else theirs, frame),
            (blocks[frame],),
            key_weight,
            value_weight_t,
            groups,
        )


def split3(x):
    high = x.astype(bf16).astype(f32)
    middle = (x - high).astype(bf16).astype(f32)
    return [high, middle, x - high - middle]


def merged(mine, theirs, frame):
    top_a, top_b = mine[frame, C2 + 8 :, :], theirs[frame, C2 + 8 :, :]
    top = jnp.maximum(top_a, top_b)
    scale_a, scale_b = jnp.exp(top_a - top), jnp.exp(top_b - top)
    mass = mine[frame, C2 : C2 + 8, :] * scale_a + theirs[frame, C2 : C2 + 8, :] * scale_b
    return mass, top, scale_a, scale_b


def merge_keep_kernel(mine, theirs, state):
    for frame in range(2):
        mass, top, scale_a, scale_b = merged(mine, theirs, frame)
        state[frame, :C2, :] = mine[frame, :C2, :] * scale_a[:1] + theirs[frame, :C2, :] * scale_b[:1]
        state[frame, C2 : C2 + 8, :] = mass
        state[frame, C2 + 8 :, :] = top


def merge_send_kernel(mine, theirs, send):
    for frame in range(2):
        mass, top, scale_a, scale_b = merged(mine, theirs, frame)
        inverse = 1.0 / mass
        scale_a, scale_b = scale_a * inverse, scale_b * inverse
        total = mine[frame, :C2, :] * scale_a[:1] + theirs[frame, :C2, :] * scale_b[:1]
        send[frame, :C2, :] = total.astype(bf16)
        rows = split3(top[:1]) + split3(mass[:1]) + [jnp.zeros((10, C2), f32)]
        send[frame, C2:, :] = jnp.concatenate(rows, axis=0).astype(bf16)


def last_kernel(reduced, state, received, weight, out):
    for frame in range(2):
        rows = received[frame, C2:, :].astype(f32)
        top_a, mass_a = state[frame, C2 + 8 : C2 + 9, :], state[frame, C2 : C2 + 1, :]
        top_b = rows[0:1] + rows[1:2] + rows[2:3]
        mass_b = rows[3:4] + rows[4:5] + rows[5:6]
        top = jnp.maximum(top_a, top_b)
        scale_a = jnp.exp(top_a - top)
        scale_b = jnp.exp(top_b - top) * mass_b
        inverse = 1.0 / (mass_a * scale_a + scale_b)
        attended = state[frame, :C2, :] * (scale_a * inverse)
        attended += received[frame, :C2, :].astype(f32) * (scale_b * inverse)
        mixed = lax.dot_general(
            attended.astype(bf16), weight[...], (((0,), (0,)), ((), ())), preferred_element_type=f32
        )
        out[frame] = reduced[frame] + mixed


def body(
    video,
    norm_gain,
    conv_weight,
    conv_bias,
    down_weight,
    down_bias,
    attention_gain,
    query_weight,
    key_weight,
    value_weight,
    output_weight,
):
    space = lax.axis_size("space")
    times = lax.axis_size("tm")
    place = lax.axis_index("space")
    has = [lax.axis_index("tm") > 0, place > 0, place < space - 1]
    flags = jnp.stack(has).astype(f32)
    scalar = {0: SMEM}

    def next_frames(x):
        return lax.ppermute(x, "tm", [(i, (i + 1) % times) for i in range(times)])

    def along(x, distance):
        return lax.ppermute(x, "space", [(i, (i + distance) % space) for i in range(space)])

    def diagonal(x, distance):
        route = [
            (t * space + i, ((t + 1) % times) * space + (i + distance) % space)
            for t in range(times)
            for i in range(space)
        ]
        return lax.ppermute(x, ("tm", "space"), route)

    def swap(x, bit):
        return lax.ppermute(x, "space", [(i, i ^ bit) for i in range(space)])

    bottom, top = call(
        edge_kernel,
        [((2, 1, COLS, C1), bf16), ((2, 2, COLS, C1), bf16)],
        [video],
        [pltpu.SemaphoreType.DMA((2,))],
        {0: HBM},
        nbytes=400_000,
    )
    above = along(bottom, 1)
    below = along(top, -1)
    halo = next_frames(video)
    far_above, far_below = diagonal(bottom, 1), diagonal(top, -1)

    square = (C2, C2)
    taps = pltpu.VMEM((3, (ROWS + 3) * COLS, C2), bf16)
    whole = ((SIZE, C2), f32)
    prepared = (3, 3) + square
    (
        acc, now, before, down_weight, query_weight, key_weight, value_weight, output_weight,
        gain, down_bias, attention_gain,
    ) = call(
        own_kernel,
        [whole, (prepared, bf16), (prepared, bf16), (down_weight.shape, bf16)]
        + [(square, bf16)] * 4
        + [((1, C1), f32), ((1, C2), f32), ((1, C2), f32)],
        [video, norm_gain.reshape(1, C1), conv_bias.reshape(1, C1), conv_weight, down_weight]
        + [query_weight, key_weight, value_weight, output_weight]
        + [down_bias.reshape(1, C2), attention_gain.reshape(1, C2)],
        [
            taps,
            pltpu.VMEM(video.shape, bf16),
            pltpu.VMEM((1, C1), f32),
            pltpu.VMEM(conv_weight.shape, bf16),
            pltpu.VMEM(square, bf16),
            pltpu.SemaphoreType.DMA((11,)),
        ],
        {i: HBM for i in range(11)},
        flops=2 * 9 * SIZE * 256 * 256,
        nbytes=6_000_000,
    )
    (acc,) = call(
        halo_kernel,
        [whole],
        [flags, acc, halo, gain, before],
        [taps],
        scalar,
        flops=2 * 9 * SIZE * 256 * 256,
        nbytes=5_000_000,
    )
    send, half_taps = call(
        sum_kernel,
        [((2, QUERIES, C2), bf16), ((3, 9 * HALF, C2), bf16)],
        [flags, acc, above, below, far_above, far_below, gain, now, before, down_weight],
        [pltpu.VMEM((3, 6 * COLS, C2), bf16), pltpu.VMEM((2, SIZE, C1), f32)],
        scalar,
        flops=2 * 18 * 256 * 256 * 256,
        nbytes=5_000_000,
    )
    received = next_frames(send)
    (part,) = call(
        down_kernel,
        [((2, QUERIES, C2), f32)],
        [half_taps, down_weight, down_bias],
        flops=2 * 18 * 256 * 256 * 256,
        nbytes=3_000_000,
    )
    pixels = ((2, QUERIES, C2), bf16)
    reduced, normed, own = call(
        norm_kernel,
        [((2, QUERIES, C2), f32), pixels, pixels],
        [flags, part, received, attention_gain, query_weight],
        spaces=scalar,
        nbytes=2_000_000,
    )
    plus, minus = [along(normed, 4)], [along(normed, -4)]
    for step in range(2):
        plus.append(along(plus[step], 4))
        minus.append(along(minus[step], -4))
    sibling, across = swap(own, 1), swap(own, 2)
    both = swap(across, 1)
    state = [((GROUPS, STATE, C2), f32)]
    flops = 2 * QUERIES * 256 * (512 + 2 * GROUPS * QUERIES)
    carry, queries = [0, 0], [0, 0]
    weights = [key_weight, value_weight]
    for frame in range(2):
        queries[frame], carry[frame] = call(
            lambda *refs: first_attend_kernel(frame, *refs),
            [((GROUPS, QUERIES, C2), bf16)] + state,
            [own, sibling, across, both, normed, plus[0], minus[0]] + weights,
            flops=3 * flops,
            nbytes=4_000_000,
        )
    def step_on(step):
        for frame in range(2):
            (carry[frame],) = call(
                lambda *refs: attend_kernel(frame, *refs),
                state,
                [queries[frame], carry[frame], plus[step], minus[step]] + weights,
                aliases={1: 0},
                flops=2 * flops,
                nbytes=4_000_000,
            )

    step_on(1)
    (plus[2], minus[2]), carry = lax.optimization_barrier(((plus[2], minus[2]), carry))
    ends = call(cut_kernel, [((QUERIES, C2), bf16)] * 2, [plus[2], minus[2]], nbytes=500_000)
    ends = [along(ends[0], 4), along(ends[1], -4)]
    step_on(2)
    pair = ((2, STATE, C2), f32)

    def finish(groups):
        mine, theirs = call(
            lambda *refs: last_attend_kernel(groups, *refs),
            [pair, pair],
            [*queries, *carry, *ends] + weights,
            flops=flops,
            nbytes=4_000_000,
        )
        return mine, swap(theirs, 1)

    (give,) = call(
        merge_send_kernel, [((2, STATE, C2), bf16)], list(finish((2, 3))), nbytes=1_500_000
    )
    received = swap(give, 2)
    (kept,) = call(merge_keep_kernel, [pair], list(finish((0, 1))), nbytes=2_000_000)
    (encoded,) = call(
        last_kernel,
        [((2, QUERIES, C2), f32)],
        [reduced, kept, received, output_weight],
        nbytes=2_000_000,
    )
    return encoded.reshape(2, ROWS // 2, HALF, C2)


def solution(mesh):
    in_specs = (P("tm", "space", None, None), P(), P(), P(), P(), P(), P(), P(), P(), P(), P())
    out_specs = P("tm", "space", None, None)
    return jax.shard_map(body, mesh=mesh, in_specs=in_specs, out_specs=out_specs, check_vma=False)
```

```python
import jax
import jax.numpy as jnp
from jax import lax
from jax.experimental import pallas as pl
from jax.experimental.pallas import tpu as pltpu
from jax.sharding import PartitionSpec as P

epsilon = 1e-05
f32 = jnp.float32
bf16 = jnp.bfloat16
VMEM = pl.BlockSpec(memory_space=pltpu.VMEM)
SMEM = pl.BlockSpec(memory_space=pltpu.SMEM)
HBM = pl.BlockSpec(memory_space=pltpu.HBM)
COLS = 128
C1 = 128
C2 = 256
ROWS = 8
HALF = 64
QUERIES = 256


def call(kernel, outs, ins, scratch=(), spaces=None, aliases=None, flops=0, nbytes=0):
    spaces = spaces or {}
    ins = [
        pltpu.with_memory_space_constraint(x, pltpu.HBM) if spaces.get(i) is HBM else x
        for i, x in enumerate(ins)
    ]
    return pl.pallas_call(
        kernel,
        out_shape=[jax.ShapeDtypeStruct(s, d) for s, d in outs],
        in_specs=[spaces.get(i, VMEM) for i in range(len(ins))],
        out_specs=[VMEM] * len(outs),
        scratch_shapes=list(scratch),
        input_output_aliases=aliases or {},
        compiler_params=pltpu.CompilerParams(vmem_limit_bytes=24 * 1024 * 1024),
        cost_estimate=pl.CostEstimate(flops=flops, bytes_accessed=nbytes, transcendentals=0),
    )(*ins)


def dot(a, b):
    return jnp.dot(a, b, preferred_element_type=f32)


def dot_t(a, b):
    return lax.dot_general(a, b, (((1,), (1,)), ((), ())), preferred_element_type=f32)


def averaging():
    i = lax.broadcasted_iota(jnp.int32, (2 * C1, 2 * C1), 0) // C1
    j = lax.broadcasted_iota(jnp.int32, (2 * C1, 2 * C1), 1) // C1
    return jnp.where(i == j, 1.0 / C1, 0.0).astype(bf16)


def activate(pair, gain2, mean_of):
    centred = pair.astype(f32) - dot(pair, mean_of)
    squares = centred * centred
    high = squares.astype(bf16)
    low = (squares - high.astype(f32)).astype(bf16)
    spread = dot(high, mean_of) + dot(low, mean_of)
    y = centred * lax.rsqrt(spread + epsilon) * gain2
    return y / (1.0 + jnp.exp(-y))


def store_shifted(taps, row, act):
    col = lax.broadcasted_iota(jnp.int32, act.shape, 0)
    at = pl.ds(row * COLS, COLS)
    taps[0, at, :] = jnp.where(col == 0, 0.0, pltpu.roll(act, 1, 0)).astype(bf16)
    taps[1, at, :] = act.astype(bf16)
    taps[2, at, :] = jnp.where(col == COLS - 1, 0.0, pltpu.roll(act, COLS - 1, 0)).astype(bf16)


def pair_of(ref, i):
    return jnp.concatenate([ref[0, i], ref[1, i]], axis=1)


def fill_taps(taps, rows, gain_ref, batch):
    gain2 = jnp.concatenate([gain_ref[...], gain_ref[...]], axis=1)
    mean_of = averaging()
    for start in range(0, len(rows), batch):
        some = rows[start : start + batch]
        pairs = jnp.concatenate([pair_of(ref, i) for _, ref, i, _ in some], axis=0)
        acts = activate(pairs, gain2, mean_of)
        for place, (row, _, _, factor) in enumerate(some):
            act = acts[place * COLS : (place + 1) * COLS]
            store_shifted(taps, row, act if factor is None else act * factor)


SIZE = (ROWS + 1) * COLS


def conv1_taps(taps, weight, acc, base):
    for kr, out, row, count in ((1, 0, 0, ROWS), (0, 1, 0, ROWS), (2, 0, 1, ROWS - 1)):
        tile = jnp.concatenate(
            [taps[kc, row * COLS : (row + count) * COLS, :] for kc in range(3)], axis=1
        )
        part = dot(tile, weight[kr].reshape(3 * C2, C2))
        at = pl.ds(out * COLS, count * COLS)
        if kr == 1:
            rest = pl.ds(ROWS * COLS, COLS)
            acc[at, :] = base(at) + part
            acc[rest, :] = base(rest)
        else:
            acc[at, :] += part


def stack(a, b, c, d):
    return jnp.concatenate([jnp.concatenate([a, b], axis=1), jnp.concatenate([c, d], axis=1)], axis=0)


def edge_kernel(video, bottom, top, sem):
    copies = [
        pltpu.make_async_copy(video.at[:, ROWS - 1 : ROWS], bottom, sem.at[0]),
        pltpu.make_async_copy(video.at[:, 0:2], top, sem.at[1]),
    ]
    for copy in copies:
        copy.start()
    for copy in copies:
        copy.wait()


def own_kernel(
    video_h, gain_h, bias_h, conv_h, down_h, query_h, key_h, value_h, output_h, down_bias_h, attention_gain_h,
    acc, now, before, down, query, key, value_t, output, gain, down_bias, attention_gain,
    taps, video, bias, conv, value, sem,
):
    pairs = (
        (gain_h, gain), (video_h, video), (bias_h, bias), (conv_h, conv), (value_h, value), (down_h, down),
        (query_h, query), (key_h, key), (output_h, output),
        (down_bias_h, down_bias), (attention_gain_h, attention_gain),
    )
    copies = [pltpu.make_async_copy(src, dst, sem.at[i]) for i, (src, dst) in enumerate(pairs)]
    for copy in copies:
        copy.start()
    for copy in copies[:3]:
        copy.wait()
    fill_taps(taps, [(row, video, row, None) for row in range(ROWS)], gain, 4)
    copies[3].wait()
    none = jnp.zeros((C1, C1), bf16)
    for kr in range(3):
        for kc in range(3):
            w0, w1, w2 = (conv[kt, kr, kc] for kt in range(3))
            now[kr, kc] = stack(w2, w1, none, w2)
            before[kr, kc] = stack(w0, none, w1, w0)

    def base(at):
        bias2 = jnp.concatenate([bias[...], bias[...]], axis=1)
        if at.start:
            return jnp.broadcast_to(bias2, (COLS, C2))
        return jnp.concatenate([pair_of(video, i).astype(f32) for i in range(ROWS)], axis=0) + bias2

    conv1_taps(taps, now, acc, base)
    copies[4].wait()
    value_t[...] = value[...].astype(f32).T.astype(bf16)
    for copy in copies[5:]:
        copy.wait()


def halo_kernel(flags, acc_in, halo, gain, weight, acc, taps):
    fill_taps(taps, [(row, halo, row, flags[0]) for row in range(ROWS)], gain, 4)
    conv1_taps(taps, weight, acc, lambda at: acc_in[at, :])


TAPS = [(kr, kc) for kr in range(3) for kc in range(3)]


def down_taps(half_taps, lanes):
    starts = (0, 5 * HALF, HALF)
    tiles = [half_taps[kc, starts[kr] : starts[kr] + QUERIES, lanes] for kr, kc in TAPS]
    return jnp.concatenate(tiles, axis=1)


def down_weights(down, times):
    return jnp.concatenate([down[kt, kr, kc] for kr, kc in TAPS for kt in times], axis=0)


def sum_kernel(
    flags, acc, above, below, far_above, far_below, gain, now, before, down,
    send, half_taps, taps, wide,
):
    past = flags[0]
    edges = [(0, above, 0, flags[1]), (1, below, 0, flags[2]), (2, below, 1, flags[2])]
    far = [(3, far_above, 0, flags[1]), (4, far_below, 0, flags[2]), (5, far_below, 1, flags[2])]
    fill_taps(taps, edges + [(row, ref, i, factor * past) for row, ref, i, factor in far], gain, 3)

    def extra(kr, row, count):
        tile = jnp.concatenate(
            [
                taps[kc, (base + row) * COLS : (base + row + count) * COLS, :]
                for base in (0, 3)
                for kc in range(3)
            ],
            axis=1,
        )
        weight = jnp.concatenate([now[kr].reshape(3 * C2, C2), before[kr].reshape(3 * C2, C2)], axis=0)
        return dot(tile, weight)

    last = extra(2, 1, 2)
    extras = {0: extra(0, 0, 1), ROWS - 1: last[:COLS]}
    extras[ROWS] = last[COLS:] + extra(1, 1, 1) + pair_of(below, 0).astype(f32)
    for row in range(ROWS + 1):
        at = pl.ds(row * COLS, COLS)
        summed = acc[at, :] + extras[row] if row in extras else acc[at, :]
        summed = summed.astype(bf16).astype(f32)
        if row == ROWS:
            summed = summed * flags[2]
        wide[0, at, :] = summed[:, :C1]
        wide[1, at, :] = summed[:, C1:]
    j = lax.broadcasted_iota(jnp.int32, (HALF, C1), 0)
    for row in range(ROWS + 1):
        place = row // 2 if row % 2 == 0 else 5 + row // 2
        for frame in range(2):
            even = wide[frame, pl.ds(row * COLS, HALF, stride=2), :]
            odd = wide[frame, pl.ds(row * COLS + 1, HALF, stride=2), :]
            after = jnp.where(j == HALF - 1, 0.0, pltpu.roll(even, HALF - 1, 0))
            lanes = pl.ds(frame * C1, C1)
            at = pl.ds(place * HALF, HALF)
            half_taps[0, at, lanes] = even.astype(bf16)
            half_taps[1, at, lanes] = odd.astype(bf16)
            half_taps[2, at, lanes] = after.astype(bf16)
    send[0] = dot(down_taps(half_taps, slice(None)), down_weights(down, (0, 1))).astype(bf16)
    send[1] = dot(down_taps(half_taps, slice(C1, None)), down_weights(down, (0,))).astype(bf16)


def down_kernel(half_taps, down, bias, out):
    out[0] = dot(down_taps(half_taps, slice(0, C1)), down_weights(down, (2,))) + bias[...]
    out[1] = dot(down_taps(half_taps, slice(None)), down_weights(down, (1, 2))) + bias[...]


def norm_kernel(flags, part, received, gain, query_weight, reduced, normed, queries):
    value = part[...] + received[...].astype(f32) * flags[0]
    reduced[...] = value
    centred = value - jnp.mean(value, axis=2, keepdims=True)
    spread = jnp.mean(centred * centred, axis=2, keepdims=True)
    result = (centred * lax.rsqrt(spread + epsilon) * gain[...]).astype(bf16)
    normed[...] = result
    for frame in range(2):
        queries[frame] = (dot(result[frame], query_weight[...]).astype(bf16) * (C2**-0.5)).astype(bf16)


GROUPS = 4
STATE = C2 + 16


def attend(queries, before, outs, blocks, key_weight, value_weight_t, groups=range(4)):
    normed = jnp.concatenate([block[...] for block in blocks], axis=0)
    keys = dot(normed, key_weight[...]).astype(bf16)
    values = dot_t(value_weight_t[...], normed).astype(bf16)
    values = jnp.concatenate([values, jnp.ones((16, values.shape[1]), bf16)], axis=0)
    ahead = dot_t(keys, queries[groups[0]])
    for i, group in enumerate(groups):
        scores = ahead
        if i + 1 < len(groups):
            ahead = dot_t(keys, queries[groups[i + 1]])
        highest = jnp.max(scores, axis=0, keepdims=True)
        if before is not None:
            old = before[group, C2 + 8 : C2 + 9, :]
            highest = jnp.maximum(old, highest)
            rescale = jnp.exp(old - highest)
        weights = jnp.exp(scores - highest).astype(bf16)
        product = dot(values, weights)[: C2 + 8]
        if before is not None:
            product += before[group, : C2 + 8, :] * rescale
        out, place = outs(group)
        out[place, : C2 + 8, :] = product
        out[place, C2 + 8 :, :] = jnp.broadcast_to(highest, (8, C2))


def early_attend_kernel(frame, own, across, block, plus, minus, key_weight, value_weight_t, state):
    blocks = [ref.at[frame] for ref in (block, plus, minus)]
    queries = {0: own[frame], 1: across[frame]}
    attend(queries, None, lambda g: (state, g), blocks, key_weight, value_weight_t, (0, 1))


def first_attend_kernel(
    frame, own, sibling, across, both, early, block, plus, minus, key_weight, value_weight_t, queries, state
):
    for group, source in enumerate((own, sibling, across, both)):
        queries[group] = source[frame]
    state[0] = early[0]
    state[2] = early[1]
    blocks = [ref.at[frame] for ref in (block, plus, minus)]
    attend(queries, None, lambda g: (state, g), blocks, key_weight, value_weight_t, (1, 3))


def attend_kernel(frame, queries, before, plus, minus, key_weight, value_weight_t, state):
    blocks = [ref.at[frame] for ref in (plus, minus)]
    attend(queries, before, lambda g: (state, g), blocks, key_weight, value_weight_t)


def cut_kernel(plus, minus, first, second):
    first[...] = plus[0]
    second[...] = minus[1]


def last_attend_kernel(groups, *refs):
    queries, before, blocks = refs[0:2], refs[2:4], refs[4:6]
    key_weight, value_weight_t, mine, theirs = refs[6:]
    for frame in range(2):
        attend(
            queries[frame],
            before[frame],
            lambda g: (mine if g == groups[0] else theirs, frame),
            (blocks[frame],),
            key_weight,
            value_weight_t,
            groups,
        )


def split3(x):
    high = x.astype(bf16).astype(f32)
    middle = (x - high).astype(bf16).astype(f32)
    return [high, middle, x - high - middle]


def merged(mine, theirs, frame):
    top_a, top_b = mine[frame, C2 + 8 :, :], theirs[frame, C2 + 8 :, :]
    top = jnp.maximum(top_a, top_b)
    scale_a, scale_b = jnp.exp(top_a - top), jnp.exp(top_b - top)
    mass = mine[frame, C2 : C2 + 8, :] * scale_a + theirs[frame, C2 : C2 + 8, :] * scale_b
    return mass, top, scale_a, scale_b


def merge_keep_kernel(mine, theirs, state):
    for frame in range(2):
        mass, top, scale_a, scale_b = merged(mine, theirs, frame)
        state[frame, :C2, :] = mine[frame, :C2, :] * scale_a[:1] + theirs[frame, :C2, :] * scale_b[:1]
        state[frame, C2 : C2 + 8, :] = mass
        state[frame, C2 + 8 :, :] = top


def merge_send_kernel(mine, theirs, send):
    for frame in range(2):
        mass, top, scale_a, scale_b = merged(mine, theirs, frame)
        inverse = 1.0 / mass
        scale_a, scale_b = scale_a * inverse, scale_b * inverse
        total = mine[frame, :C2, :] * scale_a[:1] + theirs[frame, :C2, :] * scale_b[:1]
        send[frame, :C2, :] = total.astype(bf16)
        rows = split3(top[:1]) + split3(mass[:1]) + [jnp.zeros((10, C2), f32)]
        send[frame, C2:, :] = jnp.concatenate(rows, axis=0).astype(bf16)


def last_kernel(reduced, state, received, weight, out):
    for frame in range(2):
        rows = received[frame, C2:, :].astype(f32)
        top_a, mass_a = state[frame, C2 + 8 : C2 + 9, :], state[frame, C2 : C2 + 1, :]
        top_b = rows[0:1] + rows[1:2] + rows[2:3]
        mass_b = rows[3:4] + rows[4:5] + rows[5:6]
        top = jnp.maximum(top_a, top_b)
        scale_a = jnp.exp(top_a - top)
        scale_b = jnp.exp(top_b - top) * mass_b
        inverse = 1.0 / (mass_a * scale_a + scale_b)
        attended = state[frame, :C2, :] * (scale_a * inverse)
        attended += received[frame, :C2, :].astype(f32) * (scale_b * inverse)
        mixed = lax.dot_general(
            attended.astype(bf16), weight[...], (((0,), (0,)), ((), ())), preferred_element_type=f32
        )
        out[frame] = reduced[frame] + mixed


def body(
    video,
    norm_gain,
    conv_weight,
    conv_bias,
    down_weight,
    down_bias,
    attention_gain,
    query_weight,
    key_weight,
    value_weight,
    output_weight,
):
    space = lax.axis_size("space")
    times = lax.axis_size("tm")
    place = lax.axis_index("space")
    has = [lax.axis_index("tm") > 0, place > 0, place < space - 1]
    flags = jnp.stack(has).astype(f32)
    scalar = {0: SMEM}

    def next_frames(x):
        return lax.ppermute(x, "tm", [(i, (i + 1) % times) for i in range(times)])

    def along(x, distance):
        return lax.ppermute(x, "space", [(i, (i + distance) % space) for i in range(space)])

    def diagonal(x, distance):
        route = [
            (t * space + i, ((t + 1) % times) * space + (i + distance) % space)
            for t in range(times)
            for i in range(space)
        ]
        return lax.ppermute(x, ("tm", "space"), route)

    def swap(x, bit):
        return lax.ppermute(x, "space", [(i, i ^ bit) for i in range(space)])

    bottom, top = call(
        edge_kernel,
        [((2, 1, COLS, C1), bf16), ((2, 2, COLS, C1), bf16)],
        [video],
        [pltpu.SemaphoreType.DMA((2,))],
        {0: HBM},
        nbytes=400_000,
    )
    above = along(bottom, 1)
    below = along(top, -1)
    halo = next_frames(video)
    far_above, far_below = diagonal(bottom, 1), diagonal(top, -1)

    square = (C2, C2)
    taps = pltpu.VMEM((3, ROWS * COLS, C2), bf16)
    whole = ((SIZE, C2), f32)
    prepared = (3, 3) + square
    (
        acc, now, before, down_weight, query_weight, key_weight, value_weight, output_weight,
        gain, down_bias, attention_gain,
    ) = call(
        own_kernel,
        [whole, (prepared, bf16), (prepared, bf16), (down_weight.shape, bf16)]
        + [(square, bf16)] * 4
        + [((1, C1), f32), ((1, C2), f32), ((1, C2), f32)],
        [video, norm_gain.reshape(1, C1), conv_bias.reshape(1, C1), conv_weight, down_weight]
        + [query_weight, key_weight, value_weight, output_weight]
        + [down_bias.reshape(1, C2), attention_gain.reshape(1, C2)],
        [
            taps,
            pltpu.VMEM(video.shape, bf16),
            pltpu.VMEM((1, C1), f32),
            pltpu.VMEM(conv_weight.shape, bf16),
            pltpu.VMEM(square, bf16),
            pltpu.SemaphoreType.DMA((11,)),
        ],
        {i: HBM for i in range(11)},
        flops=2 * 9 * SIZE * 256 * 256,
        nbytes=6_000_000,
    )
    (acc,) = call(
        halo_kernel,
        [whole],
        [flags, acc, halo, gain, before],
        [taps],
        scalar,
        flops=2 * 9 * SIZE * 256 * 256,
        nbytes=5_000_000,
    )
    send, half_taps = call(
        sum_kernel,
        [((2, QUERIES, C2), bf16), ((3, 9 * HALF, C2), bf16)],
        [flags, acc, above, below, far_above, far_below, gain, now, before, down_weight],
        [pltpu.VMEM((3, 6 * COLS, C2), bf16), pltpu.VMEM((2, SIZE, C1), f32)],
        scalar,
        flops=2 * 18 * 256 * 256 * 256,
        nbytes=5_000_000,
    )
    received = next_frames(send)
    (part,) = call(
        down_kernel,
        [((2, QUERIES, C2), f32)],
        [half_taps, down_weight, down_bias],
        flops=2 * 18 * 256 * 256 * 256,
        nbytes=3_000_000,
    )
    pixels = ((2, QUERIES, C2), bf16)
    reduced, normed, own = call(
        norm_kernel,
        [((2, QUERIES, C2), f32), pixels, pixels],
        [flags, part, received, attention_gain, query_weight],
        spaces=scalar,
        nbytes=2_000_000,
    )
    plus, minus = [along(normed, 4)], [along(normed, -4)]
    plus.append(along(plus[0], 4))
    minus.append(along(minus[0], -4))
    sibling, across = swap(own, 1), swap(own, 2)
    both = swap(across, 1)
    state = [((GROUPS, STATE, C2), f32)]
    flops = 2 * QUERIES * 256 * (512 + 2 * GROUPS * QUERIES)
    carry, queries = [0, 0], [0, 0]
    weights = [key_weight, value_weight]
    early = [0, 0]
    for frame in range(2):
        (early[frame],) = call(
            lambda *refs: early_attend_kernel(frame, *refs),
            [((2, STATE, C2), f32)],
            [own, across, normed, plus[0], minus[0]] + weights,
            flops=2 * flops,
            nbytes=3_000_000,
        )
    (sent, other), early = lax.optimization_barrier(((plus[1], minus[1]), early))
    plus.append(along(sent, 4))
    minus.append(along(other, -4))
    for frame in range(2):
        queries[frame], carry[frame] = call(
            lambda *refs: first_attend_kernel(frame, *refs),
            [((GROUPS, QUERIES, C2), bf16)] + state,
            [own, sibling, across, both, early[frame], normed, plus[0], minus[0]] + weights,
            flops=2 * flops,
            nbytes=4_000_000,
        )

    def step_on(step, frame):
        (carry[frame],) = call(
            lambda *refs: attend_kernel(frame, *refs),
            state,
            [queries[frame], carry[frame], plus[step], minus[step]] + weights,
            aliases={1: 0},
            flops=2 * flops,
            nbytes=4_000_000,
        )

    step_on(1, 0)
    (plus[2], minus[2]), carry = lax.optimization_barrier(((plus[2], minus[2]), carry))
    ends = call(cut_kernel, [((QUERIES, C2), bf16)] * 2, [plus[2], minus[2]], nbytes=500_000)
    ends = [along(ends[0], 4), along(ends[1], -4)]
    step_on(1, 1)
    step_on(2, 0)
    step_on(2, 1)
    pair = ((2, STATE, C2), f32)

    def finish(groups):
        mine, theirs = call(
            lambda *refs: last_attend_kernel(groups, *refs),
            [pair, pair],
            [*queries, *carry, *ends] + weights,
            flops=flops,
            nbytes=4_000_000,
        )
        return mine, swap(theirs, 1)

    (give,) = call(
        merge_send_kernel, [((2, STATE, C2), bf16)], list(finish((2, 3))), nbytes=1_500_000
    )
    received = swap(give, 2)
    (kept,) = call(merge_keep_kernel, [pair], list(finish((0, 1))), nbytes=2_000_000)
    (encoded,) = call(
        last_kernel,
        [((2, QUERIES, C2), f32)],
        [reduced, kept, received, output_weight],
        nbytes=2_000_000,
    )
    return encoded.reshape(2, ROWS // 2, HALF, C2)


def solution(mesh):
    in_specs = (P("tm", "space", None, None), P(), P(), P(), P(), P(), P(), P(), P(), P(), P())
    out_specs = P("tm", "space", None, None)
    return jax.shard_map(body, mesh=mesh, in_specs=in_specs, out_specs=out_specs, check_vma=False)
```

```python
import jax
import jax.numpy as jnp
from jax import lax
from jax.experimental import pallas as pl
from jax.experimental.pallas import tpu as pltpu
from jax.sharding import PartitionSpec as P

epsilon = 1e-05
f32 = jnp.float32
bf16 = jnp.bfloat16
VMEM = pl.BlockSpec(memory_space=pltpu.VMEM)
SMEM = pl.BlockSpec(memory_space=pltpu.SMEM)
HBM = pl.BlockSpec(memory_space=pltpu.HBM)
COLS = 128
C1 = 128
C2 = 256
ROWS = 8
HALF = 64
QUERIES = 256


def call(kernel, outs, ins, scratch=(), spaces=None, aliases=None, flops=0, nbytes=0):
    spaces = spaces or {}
    ins = [
        pltpu.with_memory_space_constraint(x, pltpu.HBM) if spaces.get(i) is HBM else x
        for i, x in enumerate(ins)
    ]
    return pl.pallas_call(
        kernel,
        out_shape=[jax.ShapeDtypeStruct(s, d) for s, d in outs],
        in_specs=[spaces.get(i, VMEM) for i in range(len(ins))],
        out_specs=[VMEM] * len(outs),
        scratch_shapes=list(scratch),
        input_output_aliases=aliases or {},
        compiler_params=pltpu.CompilerParams(vmem_limit_bytes=24 * 1024 * 1024),
        cost_estimate=pl.CostEstimate(flops=flops, bytes_accessed=nbytes, transcendentals=0),
    )(*ins)


def dot(a, b):
    return jnp.dot(a, b, preferred_element_type=f32)


def dot_t(a, b):
    return lax.dot_general(a, b, (((1,), (1,)), ((), ())), preferred_element_type=f32)


def averaging():
    i = lax.broadcasted_iota(jnp.int32, (2 * C1, 2 * C1), 0) // C1
    j = lax.broadcasted_iota(jnp.int32, (2 * C1, 2 * C1), 1) // C1
    return jnp.where(i == j, 1.0 / C1, 0.0).astype(bf16)


def activate(pair, gain2, mean_of):
    centred = pair.astype(f32) - dot(pair, mean_of)
    squares = centred * centred
    high = squares.astype(bf16)
    low = (squares - high.astype(f32)).astype(bf16)
    spread = dot(high, mean_of) + dot(low, mean_of)
    y = centred * lax.rsqrt(spread + epsilon) * gain2
    return y / (1.0 + jnp.exp(-y))


def store_shifted(taps, row, act):
    col = lax.broadcasted_iota(jnp.int32, act.shape, 0)
    at = pl.ds(row * COLS, COLS)
    taps[0, at, :] = jnp.where(col == 0, 0.0, pltpu.roll(act, 1, 0)).astype(bf16)
    taps[1, at, :] = act.astype(bf16)
    taps[2, at, :] = jnp.where(col == COLS - 1, 0.0, pltpu.roll(act, COLS - 1, 0)).astype(bf16)


def pair_of(ref, i):
    return jnp.concatenate([ref[0, i], ref[1, i]], axis=1)


def fill_taps(taps, rows, gain_ref, batch):
    gain2 = jnp.concatenate([gain_ref[...], gain_ref[...]], axis=1)
    mean_of = averaging()
    for start in range(0, len(rows), batch):
        some = rows[start : start + batch]
        pairs = jnp.concatenate([pair_of(ref, i) for _, ref, i, _ in some], axis=0)
        acts = activate(pairs, gain2, mean_of)
        for place, (row, _, _, factor) in enumerate(some):
            act = acts[place * COLS : (place + 1) * COLS]
            store_shifted(taps, row, act if factor is None else act * factor)


SIZE = (ROWS + 1) * COLS


def conv1_taps(taps, weight, acc, base):
    for kr, out, row, count in ((1, 0, 0, ROWS), (0, 1, 0, ROWS), (2, 0, 1, ROWS - 1)):
        tile = jnp.concatenate(
            [taps[kc, row * COLS : (row + count) * COLS, :] for kc in range(3)], axis=1
        )
        part = dot(tile, weight[kr].reshape(3 * C2, C2))
        at = pl.ds(out * COLS, count * COLS)
        if kr == 1:
            rest = pl.ds(ROWS * COLS, COLS)
            acc[at, :] = base(at) + part
            acc[rest, :] = base(rest)
        else:
            acc[at, :] += part


def stack(a, b, c, d):
    return jnp.concatenate([jnp.concatenate([a, b], axis=1), jnp.concatenate([c, d], axis=1)], axis=0)


def edge_kernel(video, bottom, top, sem):
    copies = [
        pltpu.make_async_copy(video.at[:, ROWS - 1 : ROWS], bottom, sem.at[0]),
        pltpu.make_async_copy(video.at[:, 0:2], top, sem.at[1]),
    ]
    for copy in copies:
        copy.start()
    for copy in copies:
        copy.wait()


def own_kernel(
    video_h, gain_h, bias_h, conv_h, down_h, query_h, key_h, value_h, output_h, down_bias_h, attention_gain_h,
    acc, now, before, down, query, key, value_t, output, gain, down_bias, attention_gain,
    taps, video, bias, conv, value, sem,
):
    pairs = (
        (gain_h, gain), (video_h, video), (bias_h, bias), (conv_h, conv), (value_h, value), (down_h, down),
        (query_h, query), (key_h, key), (output_h, output),
        (down_bias_h, down_bias), (attention_gain_h, attention_gain),
    )
    copies = [pltpu.make_async_copy(src, dst, sem.at[i]) for i, (src, dst) in enumerate(pairs)]
    for copy in copies:
        copy.start()
    for copy in copies[:3]:
        copy.wait()
    fill_taps(taps, [(row, video, row, None) for row in range(ROWS)], gain, 4)
    copies[3].wait()
    none = jnp.zeros((C1, C1), bf16)
    for kr in range(3):
        for kc in range(3):
            w0, w1, w2 = (conv[kt, kr, kc] for kt in range(3))
            now[kr, kc] = stack(w2, w1, none, w2)
            before[kr, kc] = stack(w0, none, w1, w0)

    def base(at):
        bias2 = jnp.concatenate([bias[...], bias[...]], axis=1)
        if at.start:
            return jnp.broadcast_to(bias2, (COLS, C2))
        return jnp.concatenate([pair_of(video, i).astype(f32) for i in range(ROWS)], axis=0) + bias2

    conv1_taps(taps, now, acc, base)
    copies[4].wait()
    value_t[...] = value[...].astype(f32).T.astype(bf16)
    for copy in copies[5:]:
        copy.wait()


TAPS = [(kr, kc) for kr in range(3) for kc in range(3)]


def down_taps(half_taps, lanes):
    starts = (0, 5 * HALF, HALF)
    tiles = [half_taps[kc, starts[kr] : starts[kr] + QUERIES, lanes] for kr, kc in TAPS]
    return jnp.concatenate(tiles, axis=1)


def fill_half_taps(half_taps, wide, rows, value):
    for row in rows:
        at = pl.ds(row * COLS, COLS)
        summed = value(row).astype(bf16).astype(f32)
        wide[0, at, :] = summed[:, :C1]
        wide[1, at, :] = summed[:, C1:]
    j = lax.broadcasted_iota(jnp.int32, (HALF, C1), 0)
    for row in rows:
        place = row // 2 if row % 2 == 0 else 5 + row // 2
        for frame in range(2):
            even = wide[frame, pl.ds(row * COLS, HALF, stride=2), :]
            odd = wide[frame, pl.ds(row * COLS + 1, HALF, stride=2), :]
            after = jnp.where(j == HALF - 1, 0.0, pltpu.roll(even, HALF - 1, 0))
            lanes = pl.ds(frame * C1, C1)
            at = pl.ds(place * HALF, HALF)
            half_taps[0, at, lanes] = even.astype(bf16)
            half_taps[1, at, lanes] = odd.astype(bf16)
            half_taps[2, at, lanes] = after.astype(bf16)


def send_down(send, half_taps, down, places):
    def tile(lanes):
        columns = [
            jnp.concatenate([half_taps[kc, p * HALF : (p + 1) * HALF, lanes] for p in places[kr]], axis=0)
            for kr, kc in TAPS
        ]
        return jnp.concatenate(columns, axis=1)

    send[0] = dot(tile(slice(None)), down_weights(down, (0, 1))).astype(bf16)
    send[1] = dot(tile(slice(C1, None)), down_weights(down, (0,))).astype(bf16)


def down_weights(down, times):
    return jnp.concatenate([down[kt, kr, kc] for kr, kc in TAPS for kt in times], axis=0)


def halo_kernel(flags, acc_in, halo, gain, weight, down, acc, send, taps, wide, half_taps):
    fill_taps(taps, [(row, halo, row, flags[0]) for row in range(ROWS)], gain, 4)
    conv1_taps(taps, weight, acc, lambda at: acc_in[at, :])
    fill_half_taps(half_taps, wide, range(2, ROWS - 1), lambda row: acc[pl.ds(row * COLS, COLS), :])
    send_down(send, half_taps, down, ((1, 2), (6, 7), (2, 3)))


def sum_kernel(
    flags, acc, above, below, far_above, far_below, gain, now, before, down,
    send, half_taps, taps, wide,
):
    past = flags[0]
    edges = [(0, above, 0, flags[1]), (1, below, 0, flags[2]), (2, below, 1, flags[2])]
    far = [(3, far_above, 0, flags[1]), (4, far_below, 0, flags[2]), (5, far_below, 1, flags[2])]
    fill_taps(taps, edges + [(row, ref, i, factor * past) for row, ref, i, factor in far], gain, 3)

    def extra(kr, row, count):
        tile = jnp.concatenate(
            [
                taps[kc, (base + row) * COLS : (base + row + count) * COLS, :]
                for base in (0, 3)
                for kc in range(3)
            ],
            axis=1,
        )
        weight = jnp.concatenate([now[kr].reshape(3 * C2, C2), before[kr].reshape(3 * C2, C2)], axis=0)
        return dot(tile, weight)

    last = extra(2, 1, 2)
    extras = {0: extra(0, 0, 1), ROWS - 1: last[:COLS]}
    extras[ROWS] = last[COLS:] + extra(1, 1, 1) + pair_of(below, 0).astype(f32)
    def value(row):
        at = pl.ds(row * COLS, COLS)
        total = acc[at, :] + extras[row] if row in extras else acc[at, :]
        return total * flags[2] if row == ROWS else total

    fill_half_taps(half_taps, wide, range(ROWS + 1), value)
    send_down(send, half_taps, down, ((0, 3), (5, 8), (1, 4)))


def down_kernel(flags, half_taps, down, bias, inner, out):
    out[0] = dot(down_taps(half_taps, slice(0, C1)), down_weights(down, (2,))) + bias[...]
    out[1] = dot(down_taps(half_taps, slice(None)), down_weights(down, (1, 2))) + bias[...]
    at = pl.ds(HALF, 2 * HALF)
    out[:, at, :] += inner[...].astype(f32) * flags[0]


def norm_kernel(flags, part, outer, gain, query_weight, reduced, normed, queries):
    more = outer[...].astype(f32) * flags[0]
    pieces = [part[:, :HALF] + more[:, :HALF], part[:, HALF : 3 * HALF], part[:, 3 * HALF :] + more[:, HALF:]]
    value = jnp.concatenate(pieces, axis=1)
    reduced[...] = value
    centred = value - jnp.mean(value, axis=2, keepdims=True)
    spread = jnp.mean(centred * centred, axis=2, keepdims=True)
    result = (centred * lax.rsqrt(spread + epsilon) * gain[...]).astype(bf16)
    normed[...] = result
    for frame in range(2):
        queries[frame] = (dot(result[frame], query_weight[...]).astype(bf16) * (C2**-0.5)).astype(bf16)


GROUPS = 4
STATE = C2 + 16


def attend(queries, before, outs, blocks, key_weight, value_weight_t, groups=range(4)):
    normed = jnp.concatenate([block[...] for block in blocks], axis=0)
    keys = dot(normed, key_weight[...]).astype(bf16)
    values = dot_t(value_weight_t[...], normed).astype(bf16)
    values = jnp.concatenate([values, jnp.ones((16, values.shape[1]), bf16)], axis=0)
    ahead = dot_t(keys, queries[groups[0]])
    for i, group in enumerate(groups):
        scores = ahead
        if i + 1 < len(groups):
            ahead = dot_t(keys, queries[groups[i + 1]])
        highest = jnp.max(scores, axis=0, keepdims=True)
        if before is not None:
            old = before[group, C2 + 8 : C2 + 9, :]
            highest = jnp.maximum(old, highest)
            rescale = jnp.exp(old - highest)
        weights = jnp.exp(scores - highest).astype(bf16)
        product = dot(values, weights)[: C2 + 8]
        if before is not None:
            product += before[group, : C2 + 8, :] * rescale
        out, place = outs(group)
        out[place, : C2 + 8, :] = product
        out[place, C2 + 8 :, :] = jnp.broadcast_to(highest, (8, C2))


def early_attend_kernel(frame, own, across, block, plus, minus, key_weight, value_weight_t, state):
    blocks = [ref.at[frame] for ref in (block, plus, minus)]
    queries = {0: own[frame], 1: across[frame]}
    attend(queries, None, lambda g: (state, g), blocks, key_weight, value_weight_t, (0, 1))


def first_attend_kernel(
    frame, own, sibling, across, both, early, block, plus, minus, key_weight, value_weight_t, queries, state
):
    for group, source in enumerate((own, sibling, across, both)):
        queries[group] = source[frame]
    state[0] = early[0]
    state[2] = early[1]
    blocks = [ref.at[frame] for ref in (block, plus, minus)]
    attend(queries, None, lambda g: (state, g), blocks, key_weight, value_weight_t, (1, 3))


def attend_kernel(frame, queries, before, plus, minus, key_weight, value_weight_t, state):
    blocks = [ref.at[frame] for ref in (plus, minus)]
    attend(queries, before, lambda g: (state, g), blocks, key_weight, value_weight_t)


def cut_kernel(plus, minus, first, second):
    first[...] = plus[0]
    second[...] = minus[1]


def last_attend_kernel(groups, *refs):
    queries, before, blocks = refs[0:2], refs[2:4], refs[4:6]
    key_weight, value_weight_t, mine, theirs = refs[6:]
    for frame in range(2):
        attend(
            queries[frame],
            before[frame],
            lambda g: (mine if g == groups[0] else theirs, frame),
            (blocks[frame],),
            key_weight,
            value_weight_t,
            groups,
        )


def split3(x):
    high = x.astype(bf16).astype(f32)
    middle = (x - high).astype(bf16).astype(f32)
    return [high, middle, x - high - middle]


def merged(mine, theirs, frame):
    top_a, top_b = mine[frame, C2 + 8 :, :], theirs[frame, C2 + 8 :, :]
    top = jnp.maximum(top_a, top_b)
    scale_a, scale_b = jnp.exp(top_a - top), jnp.exp(top_b - top)
    mass = mine[frame, C2 : C2 + 8, :] * scale_a + theirs[frame, C2 : C2 + 8, :] * scale_b
    return mass, top, scale_a, scale_b


def merge_keep_kernel(mine, theirs, state):
    for frame in range(2):
        mass, top, scale_a, scale_b = merged(mine, theirs, frame)
        state[frame, :C2, :] = mine[frame, :C2, :] * scale_a[:1] + theirs[frame, :C2, :] * scale_b[:1]
        state[frame, C2 : C2 + 8, :] = mass
        state[frame, C2 + 8 :, :] = top


def merge_send_kernel(mine, theirs, send):
    for frame in range(2):
        mass, top, scale_a, scale_b = merged(mine, theirs, frame)
        inverse = 1.0 / mass
        scale_a, scale_b = scale_a * inverse, scale_b * inverse
        total = mine[frame, :C2, :] * scale_a[:1] + theirs[frame, :C2, :] * scale_b[:1]
        send[frame, :C2, :] = total.astype(bf16)
        rows = split3(top[:1]) + split3(mass[:1]) + [jnp.zeros((10, C2), f32)]
        send[frame, C2:, :] = jnp.concatenate(rows, axis=0).astype(bf16)


def last_kernel(reduced, state, received, weight, out):
    for frame in range(2):
        rows = received[frame, C2:, :].astype(f32)
        top_a, mass_a = state[frame, C2 + 8 : C2 + 9, :], state[frame, C2 : C2 + 1, :]
        top_b = rows[0:1] + rows[1:2] + rows[2:3]
        mass_b = rows[3:4] + rows[4:5] + rows[5:6]
        top = jnp.maximum(top_a, top_b)
        scale_a = jnp.exp(top_a - top)
        scale_b = jnp.exp(top_b - top) * mass_b
        inverse = 1.0 / (mass_a * scale_a + scale_b)
        attended = state[frame, :C2, :] * (scale_a * inverse)
        attended += received[frame, :C2, :].astype(f32) * (scale_b * inverse)
        mixed = lax.dot_general(
            attended.astype(bf16), weight[...], (((0,), (0,)), ((), ())), preferred_element_type=f32
        )
        out[frame] = reduced[frame] + mixed


def body(
    video,
    norm_gain,
    conv_weight,
    conv_bias,
    down_weight,
    down_bias,
    attention_gain,
    query_weight,
    key_weight,
    value_weight,
    output_weight,
):
    space = lax.axis_size("space")
    times = lax.axis_size("tm")
    place = lax.axis_index("space")
    has = [lax.axis_index("tm") > 0, place > 0, place < space - 1]
    flags = jnp.stack(has).astype(f32)
    scalar = {0: SMEM}

    def next_frames(x):
        return lax.ppermute(x, "tm", [(i, (i + 1) % times) for i in range(times)])

    def along(x, distance):
        return lax.ppermute(x, "space", [(i, (i + distance) % space) for i in range(space)])

    def diagonal(x, distance):
        route = [
            (t * space + i, ((t + 1) % times) * space + (i + distance) % space)
            for t in range(times)
            for i in range(space)
        ]
        return lax.ppermute(x, ("tm", "space"), route)

    def swap(x, bit):
        return lax.ppermute(x, "space", [(i, i ^ bit) for i in range(space)])

    bottom, top = call(
        edge_kernel,
        [((2, 1, COLS, C1), bf16), ((2, 2, COLS, C1), bf16)],
        [video],
        [pltpu.SemaphoreType.DMA((2,))],
        {0: HBM},
        nbytes=400_000,
    )
    above = along(bottom, 1)
    below = along(top, -1)
    halo = next_frames(video)
    far_above, far_below = diagonal(bottom, 1), diagonal(top, -1)

    square = (C2, C2)
    taps = pltpu.VMEM((3, ROWS * COLS, C2), bf16)
    whole = ((SIZE, C2), f32)
    prepared = (3, 3) + square
    (
        acc, now, before, down_weight, query_weight, key_weight, value_weight, output_weight,
        gain, down_bias, attention_gain,
    ) = call(
        own_kernel,
        [whole, (prepared, bf16), (prepared, bf16), (down_weight.shape, bf16)]
        + [(square, bf16)] * 4
        + [((1, C1), f32), ((1, C2), f32), ((1, C2), f32)],
        [video, norm_gain.reshape(1, C1), conv_bias.reshape(1, C1), conv_weight, down_weight]
        + [query_weight, key_weight, value_weight, output_weight]
        + [down_bias.reshape(1, C2), attention_gain.reshape(1, C2)],
        [
            taps,
            pltpu.VMEM(video.shape, bf16),
            pltpu.VMEM((1, C1), f32),
            pltpu.VMEM(conv_weight.shape, bf16),
            pltpu.VMEM(square, bf16),
            pltpu.SemaphoreType.DMA((11,)),
        ],
        {i: HBM for i in range(11)},
        flops=2 * 9 * SIZE * 256 * 256,
        nbytes=6_000_000,
    )
    wide = pltpu.VMEM((2, SIZE, C1), f32)
    half = ((3, 9 * HALF, C2), bf16)
    some = ((2, QUERIES // 2, C2), bf16)
    acc, send_inner = call(
        halo_kernel,
        [whole, some],
        [flags, acc, halo, gain, before, down_weight],
        [taps, wide, pltpu.VMEM(*half)],
        scalar,
        flops=2 * 9 * SIZE * 256 * 256,
        nbytes=5_000_000,
    )
    received_inner = next_frames(send_inner)
    send, half_taps = call(
        sum_kernel,
        [some, half],
        [flags, acc, above, below, far_above, far_below, gain, now, before, down_weight],
        [pltpu.VMEM((3, 6 * COLS, C2), bf16), wide],
        scalar,
        flops=2 * 18 * 256 * 256 * 256,
        nbytes=5_000_000,
    )
    received = next_frames(send)
    (part,) = call(
        down_kernel,
        [((2, QUERIES, C2), f32)],
        [flags, half_taps, down_weight, down_bias, received_inner],
        spaces=scalar,
        flops=2 * 18 * 256 * 256 * 256,
        nbytes=3_000_000,
    )
    pixels = ((2, QUERIES, C2), bf16)
    reduced, normed, own = call(
        norm_kernel,
        [((2, QUERIES, C2), f32), pixels, pixels],
        [flags, part, received, attention_gain, query_weight],
        spaces=scalar,
        nbytes=2_000_000,
    )
    plus, minus = [along(normed, 4)], [along(normed, -4)]
    plus.append(along(plus[0], 4))
    minus.append(along(minus[0], -4))
    sibling, across = swap(own, 1), swap(own, 2)
    both = swap(across, 1)
    state = [((GROUPS, STATE, C2), f32)]
    flops = 2 * QUERIES * 256 * (512 + 2 * GROUPS * QUERIES)
    carry, queries = [0, 0], [0, 0]
    weights = [key_weight, value_weight]
    early = [0, 0]
    for frame in range(2):
        (early[frame],) = call(
            lambda *refs: early_attend_kernel(frame, *refs),
            [((2, STATE, C2), f32)],
            [own, across, normed, plus[0], minus[0]] + weights,
            flops=2 * flops,
            nbytes=3_000_000,
        )
    (sent, other), early = lax.optimization_barrier(((plus[1], minus[1]), early))
    plus.append(along(sent, 4))
    minus.append(along(other, -4))
    for frame in range(2):
        queries[frame], carry[frame] = call(
            lambda *refs: first_attend_kernel(frame, *refs),
            [((GROUPS, QUERIES, C2), bf16)] + state,
            [own, sibling, across, both, early[frame], normed, plus[0], minus[0]] + weights,
            flops=2 * flops,
            nbytes=4_000_000,
        )

    def step_on(step, frame):
        (carry[frame],) = call(
            lambda *refs: attend_kernel(frame, *refs),
            state,
            [queries[frame], carry[frame], plus[step], minus[step]] + weights,
            aliases={1: 0},
            flops=2 * flops,
            nbytes=4_000_000,
        )

    step_on(1, 0)
    (plus[2], minus[2]), carry = lax.optimization_barrier(((plus[2], minus[2]), carry))
    ends = call(cut_kernel, [((QUERIES, C2), bf16)] * 2, [plus[2], minus[2]], nbytes=500_000)
    ends = [along(ends[0], 4), along(ends[1], -4)]
    step_on(1, 1)
    step_on(2, 0)
    step_on(2, 1)
    pair = ((2, STATE, C2), f32)

    def finish(groups):
        mine, theirs = call(
            lambda *refs: last_attend_kernel(groups, *refs),
            [pair, pair],
            [*queries, *carry, *ends] + weights,
            flops=flops,
            nbytes=4_000_000,
        )
        return mine, swap(theirs, 1)

    (give,) = call(
        merge_send_kernel, [((2, STATE, C2), bf16)], list(finish((2, 3))), nbytes=1_500_000
    )
    received = swap(give, 2)
    (kept,) = call(merge_keep_kernel, [pair], list(finish((0, 1))), nbytes=2_000_000)
    (encoded,) = call(
        last_kernel,
        [((2, QUERIES, C2), f32)],
        [reduced, kept, received, output_weight],
        nbytes=2_000_000,
    )
    return encoded.reshape(2, ROWS // 2, HALF, C2)


def solution(mesh):
    in_specs = (P("tm", "space", None, None), P(), P(), P(), P(), P(), P(), P(), P(), P(), P())
    out_specs = P("tm", "space", None, None)
    return jax.shard_map(body, mesh=mesh, in_specs=in_specs, out_specs=out_specs, check_vma=False)
```

```python
import jax
import jax.numpy as jnp
from jax import lax
from jax.experimental import pallas as pl
from jax.experimental.pallas import tpu as pltpu
from jax.sharding import PartitionSpec as P

epsilon = 1e-05
f32 = jnp.float32
bf16 = jnp.bfloat16
VMEM = pl.BlockSpec(memory_space=pltpu.VMEM)
SMEM = pl.BlockSpec(memory_space=pltpu.SMEM)
HBM = pl.BlockSpec(memory_space=pltpu.HBM)
COLS = 128
C1 = 128
C2 = 256
ROWS = 8
HALF = 64
QUERIES = 256


def call(kernel, outs, ins, scratch=(), spaces=None, aliases=None, flops=0, nbytes=0, out_space=VMEM):
    spaces = spaces or {}
    ins = [
        pltpu.with_memory_space_constraint(x, pltpu.HBM) if spaces.get(i) is HBM else x
        for i, x in enumerate(ins)
    ]
    return pl.pallas_call(
        kernel,
        out_shape=[jax.ShapeDtypeStruct(s, d) for s, d in outs],
        in_specs=[spaces.get(i, VMEM) for i in range(len(ins))],
        out_specs=[out_space] * len(outs),
        scratch_shapes=list(scratch),
        input_output_aliases=aliases or {},
        compiler_params=pltpu.CompilerParams(vmem_limit_bytes=24 * 1024 * 1024),
        cost_estimate=pl.CostEstimate(flops=flops, bytes_accessed=nbytes, transcendentals=0),
    )(*ins)


def dot(a, b):
    return jnp.dot(a, b, preferred_element_type=f32)


def dot_t(a, b):
    return lax.dot_general(a, b, (((1,), (1,)), ((), ())), preferred_element_type=f32)


def averaging():
    i = lax.broadcasted_iota(jnp.int32, (2 * C1, 2 * C1), 0) // C1
    j = lax.broadcasted_iota(jnp.int32, (2 * C1, 2 * C1), 1) // C1
    return jnp.where(i == j, 1.0 / C1, 0.0).astype(bf16)


def activate(pair, gain2, mean_of):
    centred = pair.astype(f32) - dot(pair, mean_of)
    squares = centred * centred
    high = squares.astype(bf16)
    low = (squares - high.astype(f32)).astype(bf16)
    spread = dot(high, mean_of) + dot(low, mean_of)
    y = centred * lax.rsqrt(spread + epsilon) * gain2
    return y / (1.0 + jnp.exp(-y))


def store_shifted(taps, row, act):
    col = lax.broadcasted_iota(jnp.int32, act.shape, 0)
    at = pl.ds(row * COLS, COLS)
    taps[0, at, :] = jnp.where(col == 0, 0.0, pltpu.roll(act, 1, 0)).astype(bf16)
    taps[1, at, :] = act.astype(bf16)
    taps[2, at, :] = jnp.where(col == COLS - 1, 0.0, pltpu.roll(act, COLS - 1, 0)).astype(bf16)


def pair_of(ref, i):
    return jnp.concatenate([ref[0, i], ref[1, i]], axis=1)


def fill_taps(taps, rows, gain_ref, batch):
    gain2 = jnp.concatenate([gain_ref[...], gain_ref[...]], axis=1)
    mean_of = averaging()
    for start in range(0, len(rows), batch):
        some = rows[start : start + batch]
        pairs = jnp.concatenate([pair_of(ref, i) for _, ref, i, _ in some], axis=0)
        acts = activate(pairs, gain2, mean_of)
        for place, (row, _, _, factor) in enumerate(some):
            act = acts[place * COLS : (place + 1) * COLS]
            store_shifted(taps, row, act if factor is None else act * factor)


SIZE = (ROWS + 1) * COLS


def conv1_taps(taps, weight, acc, base):
    for kr, out, row, count in ((1, 0, 0, ROWS), (0, 1, 0, ROWS), (2, 0, 1, ROWS - 1)):
        tile = jnp.concatenate(
            [taps[kc, row * COLS : (row + count) * COLS, :] for kc in range(3)], axis=1
        )
        part = dot(tile, weight[kr].reshape(3 * C2, C2))
        at = pl.ds(out * COLS, count * COLS)
        if kr == 1:
            rest = pl.ds(ROWS * COLS, COLS)
            acc[at, :] = base(at) + part
            acc[rest, :] = base(rest)
        else:
            acc[at, :] += part


def stack(a, b, c, d):
    return jnp.concatenate([jnp.concatenate([a, b], axis=1), jnp.concatenate([c, d], axis=1)], axis=0)


def edge_kernel(video, bottom, top, sem):
    copies = [
        pltpu.make_async_copy(video.at[:, ROWS - 1 : ROWS], bottom, sem.at[0]),
        pltpu.make_async_copy(video.at[:, 0:2], top, sem.at[1]),
    ]
    for copy in copies:
        copy.start()
    for copy in copies:
        copy.wait()


def own_kernel(
    video_h, gain_h, bias_h, conv_h, down_h, query_h, key_h, value_h, output_h, down_bias_h, attention_gain_h,
    acc, now, before, down, query, key, value_t, output, gain, down_bias, attention_gain,
    taps, video, bias, conv, value, sem,
):
    pairs = (
        (gain_h, gain), (video_h, video), (bias_h, bias), (conv_h, conv), (value_h, value), (down_h, down),
        (query_h, query), (key_h, key), (output_h, output),
        (down_bias_h, down_bias), (attention_gain_h, attention_gain),
    )
    copies = [pltpu.make_async_copy(src, dst, sem.at[i]) for i, (src, dst) in enumerate(pairs)]
    for copy in copies:
        copy.start()
    for copy in copies[:3]:
        copy.wait()
    fill_taps(taps, [(row, video, row, None) for row in range(ROWS)], gain, 4)
    copies[3].wait()
    none = jnp.zeros((C1, C1), bf16)
    for kr in range(3):
        for kc in range(3):
            w0, w1, w2 = (conv[kt, kr, kc] for kt in range(3))
            now[kr, kc] = stack(w2, w1, none, w2)
            before[kr, kc] = stack(w0, none, w1, w0)

    def base(at):
        bias2 = jnp.concatenate([bias[...], bias[...]], axis=1)
        if at.start:
            return jnp.broadcast_to(bias2, (COLS, C2))
        return jnp.concatenate([pair_of(video, i).astype(f32) for i in range(ROWS)], axis=0) + bias2

    conv1_taps(taps, now, acc, base)
    copies[4].wait()
    value_t[...] = value[...].astype(f32).T.astype(bf16)
    for copy in copies[5:]:
        copy.wait()


TAPS = [(kr, kc) for kr in range(3) for kc in range(3)]


def down_taps(half_taps, lanes):
    starts = (0, 5 * HALF, HALF)
    tiles = [half_taps[kc, starts[kr] : starts[kr] + QUERIES, lanes] for kr, kc in TAPS]
    return jnp.concatenate(tiles, axis=1)


def fill_half_taps(half_taps, wide, rows, value):
    for row in rows:
        at = pl.ds(row * COLS, COLS)
        summed = value(row).astype(bf16).astype(f32)
        wide[0, at, :] = summed[:, :C1]
        wide[1, at, :] = summed[:, C1:]
    j = lax.broadcasted_iota(jnp.int32, (HALF, C1), 0)
    for row in rows:
        place = row // 2 if row % 2 == 0 else 5 + row // 2
        for frame in range(2):
            even = wide[frame, pl.ds(row * COLS, HALF, stride=2), :]
            odd = wide[frame, pl.ds(row * COLS + 1, HALF, stride=2), :]
            after = jnp.where(j == HALF - 1, 0.0, pltpu.roll(even, HALF - 1, 0))
            lanes = pl.ds(frame * C1, C1)
            at = pl.ds(place * HALF, HALF)
            half_taps[0, at, lanes] = even.astype(bf16)
            half_taps[1, at, lanes] = odd.astype(bf16)
            half_taps[2, at, lanes] = after.astype(bf16)


def send_down(send, half_taps, down, places):
    def tile(lanes):
        columns = [
            jnp.concatenate([half_taps[kc, p * HALF : (p + 1) * HALF, lanes] for p in places[kr]], axis=0)
            for kr, kc in TAPS
        ]
        return jnp.concatenate(columns, axis=1)

    send[0] = dot(tile(slice(None)), down_weights(down, (0, 1))).astype(bf16)
    send[1] = dot(tile(slice(C1, None)), down_weights(down, (0,))).astype(bf16)


def down_weights(down, times):
    return jnp.concatenate([down[kt, kr, kc] for kr, kc in TAPS for kt in times], axis=0)


def halo_kernel(flags, acc_in, halo, gain, weight, down, acc, send, taps, wide, half_taps):
    fill_taps(taps, [(row, halo, row, flags[0]) for row in range(ROWS)], gain, 4)
    conv1_taps(taps, weight, acc, lambda at: acc_in[at, :])
    fill_half_taps(half_taps, wide, range(2, ROWS - 1), lambda row: acc[pl.ds(row * COLS, COLS), :])
    send_down(send, half_taps, down, ((1, 2), (6, 7), (2, 3)))


def sum_kernel(
    flags, acc, above, below, far_above, far_below, gain, now, before, down,
    send, half_taps, taps, wide,
):
    past = flags[0]
    edges = [(0, above, 0, flags[1]), (1, below, 0, flags[2]), (2, below, 1, flags[2])]
    far = [(3, far_above, 0, flags[1]), (4, far_below, 0, flags[2]), (5, far_below, 1, flags[2])]
    fill_taps(taps, edges + [(row, ref, i, factor * past) for row, ref, i, factor in far], gain, 3)

    def extra(kr, row, count):
        tile = jnp.concatenate(
            [
                taps[kc, (base + row) * COLS : (base + row + count) * COLS, :]
                for base in (0, 3)
                for kc in range(3)
            ],
            axis=1,
        )
        weight = jnp.concatenate([now[kr].reshape(3 * C2, C2), before[kr].reshape(3 * C2, C2)], axis=0)
        return dot(tile, weight)

    last = extra(2, 1, 2)
    extras = {0: extra(0, 0, 1), ROWS - 1: last[:COLS]}
    extras[ROWS] = last[COLS:] + extra(1, 1, 1) + pair_of(below, 0).astype(f32)
    def value(row):
        at = pl.ds(row * COLS, COLS)
        total = acc[at, :] + extras[row] if row in extras else acc[at, :]
        return total * flags[2] if row == ROWS else total

    fill_half_taps(half_taps, wide, range(ROWS + 1), value)
    send_down(send, half_taps, down, ((0, 3), (5, 8), (1, 4)))


def normalise(value, gain, query_weight):
    centred = value - jnp.mean(value, axis=2, keepdims=True)
    spread = jnp.mean(centred * centred, axis=2, keepdims=True)
    result = (centred * lax.rsqrt(spread + epsilon) * gain[...]).astype(bf16)
    query = [(dot(result[i], query_weight[...]).astype(bf16) * (C2**-0.5)).astype(bf16) for i in range(2)]
    return result, query


INNER = slice(HALF, 3 * HALF)


def down_kernel(flags, half_taps, down, bias, inner, gain, query_weight, out, normed, queries):
    out[0] = dot(down_taps(half_taps, slice(0, C1)), down_weights(down, (2,))) + bias[...]
    out[1] = dot(down_taps(half_taps, slice(None)), down_weights(down, (1, 2))) + bias[...]
    value = out[:, INNER, :] + inner[...].astype(f32) * flags[0]
    out[:, INNER, :] = value
    normed[...], query = normalise(value, gain, query_weight)
    queries[0], queries[1] = query


def norm_kernel(
    flags, part, outer, inner_normed, inner_queries, gain, query_weight, reduced, normed, queries
):
    value = jnp.concatenate([part[:, :HALF], part[:, 3 * HALF :]], axis=1)
    value = value + outer[...].astype(f32) * flags[0]
    result, query = normalise(value, gain, query_weight)
    for frame in range(2):
        for ref, edge, middle in (
            (reduced, value[frame], part[frame, INNER, :]),
            (normed, result[frame], inner_normed[frame]),
            (queries, query[frame], inner_queries[frame]),
        ):
            ref[frame, :HALF, :] = edge[:HALF]
            ref[frame, INNER, :] = middle
            ref[frame, 3 * HALF :, :] = edge[HALF:]


GROUPS = 4
STATE = C2 + 16


def attend(queries, before, outs, blocks, key_weight, value_weight_t, groups=range(4)):
    normed = jnp.concatenate([block[...] for block in blocks], axis=0)
    keys = dot(normed, key_weight[...]).astype(bf16)
    values = dot_t(value_weight_t[...], normed).astype(bf16)
    values = jnp.concatenate([values, jnp.ones((16, values.shape[1]), bf16)], axis=0)
    ahead = dot_t(keys, queries[groups[0]])
    for i, group in enumerate(groups):
        scores = ahead
        if i + 1 < len(groups):
            ahead = dot_t(keys, queries[groups[i + 1]])
        highest = jnp.max(scores, axis=0, keepdims=True)
        if before is not None:
            old = before[group, C2 + 8 : C2 + 9, :]
            highest = jnp.maximum(old, highest)
            rescale = jnp.exp(old - highest)
        weights = jnp.exp(scores - highest).astype(bf16)
        product = dot(values, weights)[: C2 + 8]
        if before is not None:
            product += before[group, : C2 + 8, :] * rescale
        out, place = outs(group)
        out[place, : C2 + 8, :] = product
        out[place, C2 + 8 :, :] = jnp.broadcast_to(highest, (8, C2))


def early_attend_kernel(frame, own, across, block, plus, minus, key_weight, value_weight_t, state):
    blocks = [ref.at[frame] for ref in (block, plus, minus)]
    queries = {0: own[frame], 1: across[frame]}
    attend(queries, None, lambda g: (state, g), blocks, key_weight, value_weight_t, (0, 1))


def first_attend_kernel(
    frame, own, sibling, across, both, early, block, plus, minus, key_weight, value_weight_t, queries, state
):
    for group, source in enumerate((own, sibling, across, both)):
        queries[group] = source[frame]
    state[0] = early[0]
    state[2] = early[1]
    blocks = [ref.at[frame] for ref in (block, plus, minus)]
    attend(queries, None, lambda g: (state, g), blocks, key_weight, value_weight_t, (1, 3))


def attend_kernel(frame, queries, before, plus, minus, key_weight, value_weight_t, state):
    blocks = [ref.at[frame] for ref in (plus, minus)]
    attend(queries, before, lambda g: (state, g), blocks, key_weight, value_weight_t)


def cut_kernel(plus, minus, first, second):
    first[...] = plus[0]
    second[...] = minus[1]


def last_attend_kernel(groups, *refs):
    queries, before, blocks = refs[0:2], refs[2:4], refs[4:6]
    key_weight, value_weight_t, mine, theirs = refs[6:]
    for frame in range(2):
        attend(
            queries[frame],
            before[frame],
            lambda g: (mine if g == groups[0] else theirs, frame),
            (blocks[frame],),
            key_weight,
            value_weight_t,
            groups,
        )


def split3(x):
    high = x.astype(bf16).astype(f32)
    middle = (x - high).astype(bf16).astype(f32)
    return [high, middle, x - high - middle]


def merged(mine, theirs, frame):
    top_a, top_b = mine[frame, C2 + 8 :, :], theirs[frame, C2 + 8 :, :]
    top = jnp.maximum(top_a, top_b)
    scale_a, scale_b = jnp.exp(top_a - top), jnp.exp(top_b - top)
    mass = mine[frame, C2 : C2 + 8, :] * scale_a + theirs[frame, C2 : C2 + 8, :] * scale_b
    return mass, top, scale_a, scale_b


def merge_keep_kernel(mine, theirs, state):
    for frame in range(2):
        mass, top, scale_a, scale_b = merged(mine, theirs, frame)
        state[frame, :C2, :] = mine[frame, :C2, :] * scale_a[:1] + theirs[frame, :C2, :] * scale_b[:1]
        state[frame, C2 : C2 + 8, :] = mass
        state[frame, C2 + 8 :, :] = top


def merge_send_kernel(mine, theirs, send):
    for frame in range(2):
        mass, top, scale_a, scale_b = merged(mine, theirs, frame)
        inverse = 1.0 / mass
        scale_a, scale_b = scale_a * inverse, scale_b * inverse
        total = mine[frame, :C2, :] * scale_a[:1] + theirs[frame, :C2, :] * scale_b[:1]
        send[frame, :C2, :] = total.astype(bf16)
        rows = split3(top[:1]) + split3(mass[:1]) + [jnp.zeros((10, C2), f32)]
        send[frame, C2:, :] = jnp.concatenate(rows, axis=0).astype(bf16)


def last_kernel(reduced, state, received, weight, out, held, sem):
    copies = []
    for frame in range(2):
        rows = received[frame, C2:, :].astype(f32)
        top_a, mass_a = state[frame, C2 + 8 : C2 + 9, :], state[frame, C2 : C2 + 1, :]
        top_b = rows[0:1] + rows[1:2] + rows[2:3]
        mass_b = rows[3:4] + rows[4:5] + rows[5:6]
        top = jnp.maximum(top_a, top_b)
        scale_a = jnp.exp(top_a - top)
        scale_b = jnp.exp(top_b - top) * mass_b
        inverse = 1.0 / (mass_a * scale_a + scale_b)
        attended = state[frame, :C2, :] * (scale_a * inverse)
        attended += received[frame, :C2, :].astype(f32) * (scale_b * inverse)
        mixed = lax.dot_general(
            attended.astype(bf16), weight[...], (((0,), (0,)), ((), ())), preferred_element_type=f32
        )
        held[frame] = reduced[frame] + mixed
        copies.append(pltpu.make_async_copy(held.at[frame], out.at[frame], sem.at[frame]))
        copies[frame].start()
    for copy in copies:
        copy.wait()


def body(
    video,
    norm_gain,
    conv_weight,
    conv_bias,
    down_weight,
    down_bias,
    attention_gain,
    query_weight,
    key_weight,
    value_weight,
    output_weight,
):
    space = lax.axis_size("space")
    times = lax.axis_size("tm")
    place = lax.axis_index("space")
    has = [lax.axis_index("tm") > 0, place > 0, place < space - 1]
    flags = jnp.stack(has).astype(f32)
    scalar = {0: SMEM}

    def next_frames(x):
        return lax.ppermute(x, "tm", [(i, (i + 1) % times) for i in range(times)])

    def along(x, distance):
        return lax.ppermute(x, "space", [(i, (i + distance) % space) for i in range(space)])

    def diagonal(x, distance):
        route = [
            (t * space + i, ((t + 1) % times) * space + (i + distance) % space)
            for t in range(times)
            for i in range(space)
        ]
        return lax.ppermute(x, ("tm", "space"), route)

    def swap(x, bit):
        return lax.ppermute(x, "space", [(i, i ^ bit) for i in range(space)])

    bottom, top = call(
        edge_kernel,
        [((2, 1, COLS, C1), bf16), ((2, 2, COLS, C1), bf16)],
        [video],
        [pltpu.SemaphoreType.DMA((2,))],
        {0: HBM},
        nbytes=400_000,
    )
    above = along(bottom, 1)
    below = along(top, -1)
    halo = next_frames(video)
    far_above, far_below = diagonal(bottom, 1), diagonal(top, -1)

    square = (C2, C2)
    taps = pltpu.VMEM((3, ROWS * COLS, C2), bf16)
    whole = ((SIZE, C2), f32)
    prepared = (3, 3) + square
    (
        acc, now, before, down_weight, query_weight, key_weight, value_weight, output_weight,
        gain, down_bias, attention_gain,
    ) = call(
        own_kernel,
        [whole, (prepared, bf16), (prepared, bf16), (down_weight.shape, bf16)]
        + [(square, bf16)] * 4
        + [((1, C1), f32), ((1, C2), f32), ((1, C2), f32)],
        [video, norm_gain.reshape(1, C1), conv_bias.reshape(1, C1), conv_weight, down_weight]
        + [query_weight, key_weight, value_weight, output_weight]
        + [down_bias.reshape(1, C2), attention_gain.reshape(1, C2)],
        [
            taps,
            pltpu.VMEM(video.shape, bf16),
            pltpu.VMEM((1, C1), f32),
            pltpu.VMEM(conv_weight.shape, bf16),
            pltpu.VMEM(square, bf16),
            pltpu.SemaphoreType.DMA((11,)),
        ],
        {i: HBM for i in range(11)},
        flops=2 * 9 * SIZE * 256 * 256,
        nbytes=6_000_000,
    )
    wide = pltpu.VMEM((2, SIZE, C1), f32)
    half = ((3, 9 * HALF, C2), bf16)
    some = ((2, QUERIES // 2, C2), bf16)
    acc, send_inner = call(
        halo_kernel,
        [whole, some],
        [flags, acc, halo, gain, before, down_weight],
        [taps, wide, pltpu.VMEM(*half)],
        scalar,
        flops=2 * 9 * SIZE * 256 * 256,
        nbytes=5_000_000,
    )
    received_inner = next_frames(send_inner)
    send, half_taps = call(
        sum_kernel,
        [some, half],
        [flags, acc, above, below, far_above, far_below, gain, now, before, down_weight],
        [pltpu.VMEM((3, 6 * COLS, C2), bf16), wide],
        scalar,
        flops=2 * 18 * 256 * 256 * 256,
        nbytes=5_000_000,
    )
    received = next_frames(send)
    part, *inner = call(
        down_kernel,
        [((2, QUERIES, C2), f32), some, some],
        [flags, half_taps, down_weight, down_bias, received_inner, attention_gain, query_weight],
        spaces=scalar,
        flops=2 * 18 * 256 * 256 * 256,
        nbytes=3_000_000,
    )
    pixels = ((2, QUERIES, C2), bf16)
    reduced, normed, own = call(
        norm_kernel,
        [((2, QUERIES, C2), f32), pixels, pixels],
        [flags, part, received, *inner, attention_gain, query_weight],
        spaces=scalar,
        nbytes=2_000_000,
    )
    plus, minus = [along(normed, 4)], [along(normed, -4)]
    plus.append(along(plus[0], 4))
    minus.append(along(minus[0], -4))
    sibling, across = swap(own, 1), swap(own, 2)
    both = swap(across, 1)
    state = [((GROUPS, STATE, C2), f32)]
    flops = 2 * QUERIES * 256 * (512 + 2 * GROUPS * QUERIES)
    carry, queries = [0, 0], [0, 0]
    weights = [key_weight, value_weight]
    early = [0, 0]
    for frame in range(2):
        (early[frame],) = call(
            lambda *refs: early_attend_kernel(frame, *refs),
            [((2, STATE, C2), f32)],
            [own, across, normed, plus[0], minus[0]] + weights,
            flops=2 * flops,
            nbytes=3_000_000,
        )
    (sent, other), early = lax.optimization_barrier(((plus[1], minus[1]), early))
    plus.append(along(sent, 4))
    minus.append(along(other, -4))
    for frame in range(2):
        queries[frame], carry[frame] = call(
            lambda *refs: first_attend_kernel(frame, *refs),
            [((GROUPS, QUERIES, C2), bf16)] + state,
            [own, sibling, across, both, early[frame], normed, plus[0], minus[0]] + weights,
            flops=2 * flops,
            nbytes=4_000_000,
        )

    def step_on(step, frame):
        (carry[frame],) = call(
            lambda *refs: attend_kernel(frame, *refs),
            state,
            [queries[frame], carry[frame], plus[step], minus[step]] + weights,
            aliases={1: 0},
            flops=2 * flops,
            nbytes=4_000_000,
        )

    step_on(1, 0)
    (plus[2], minus[2]), carry = lax.optimization_barrier(((plus[2], minus[2]), carry))
    ends = call(cut_kernel, [((QUERIES, C2), bf16)] * 2, [plus[2], minus[2]], nbytes=500_000)
    ends = [along(ends[0], 4), along(ends[1], -4)]
    step_on(1, 1)
    step_on(2, 0)
    step_on(2, 1)
    pair = ((2, STATE, C2), f32)

    def finish(groups):
        mine, theirs = call(
            lambda *refs: last_attend_kernel(groups, *refs),
            [pair, pair],
            [*queries, *carry, *ends] + weights,
            flops=flops,
            nbytes=4_000_000,
        )
        return mine, swap(theirs, 1)

    (give,) = call(
        merge_send_kernel, [((2, STATE, C2), bf16)], list(finish((2, 3))), nbytes=1_500_000
    )
    received = swap(give, 2)
    (kept,) = call(merge_keep_kernel, [pair], list(finish((0, 1))), nbytes=2_000_000)
    (encoded,) = call(
        last_kernel,
        [((2, QUERIES, C2), f32)],
        [reduced, kept, received, output_weight],
        [pltpu.VMEM((2, QUERIES, C2), f32), pltpu.SemaphoreType.DMA((2,))],
        out_space=HBM,
        nbytes=2_000_000,
    )
    return encoded.reshape(2, ROWS // 2, HALF, C2)


def solution(mesh):
    in_specs = (P("tm", "space", None, None), P(), P(), P(), P(), P(), P(), P(), P(), P(), P())
    out_specs = P("tm", "space", None, None)
    return jax.shard_map(body, mesh=mesh, in_specs=in_specs, out_specs=out_specs, check_vma=False)
```

```python
import jax
import jax.numpy as jnp
from jax import lax
from jax.experimental import pallas as pl
from jax.experimental.pallas import tpu as pltpu
from jax.sharding import PartitionSpec as P

epsilon = 1e-05
f32 = jnp.float32
bf16 = jnp.bfloat16
VMEM = pl.BlockSpec(memory_space=pltpu.VMEM)
SMEM = pl.BlockSpec(memory_space=pltpu.SMEM)
HBM = pl.BlockSpec(memory_space=pltpu.HBM)
COLS = 128
C1 = 128
C2 = 256
ROWS = 8
HALF = 64
QUERIES = 256


def call(kernel, outs, ins, scratch=(), spaces=None, aliases=None, flops=0, nbytes=0, out_space=VMEM):
    spaces = spaces or {}
    ins = [
        pltpu.with_memory_space_constraint(x, pltpu.HBM) if spaces.get(i) is HBM else x
        for i, x in enumerate(ins)
    ]
    return pl.pallas_call(
        kernel,
        out_shape=[jax.ShapeDtypeStruct(s, d) for s, d in outs],
        in_specs=[spaces.get(i, VMEM) for i in range(len(ins))],
        out_specs=[out_space] * len(outs),
        scratch_shapes=list(scratch),
        input_output_aliases=aliases or {},
        compiler_params=pltpu.CompilerParams(vmem_limit_bytes=24 * 1024 * 1024),
        cost_estimate=pl.CostEstimate(flops=flops, bytes_accessed=nbytes, transcendentals=0),
    )(*ins)


def dot(a, b):
    return jnp.dot(a, b, preferred_element_type=f32)


def dot_t(a, b):
    return lax.dot_general(a, b, (((1,), (1,)), ((), ())), preferred_element_type=f32)


def averaging():
    i = lax.broadcasted_iota(jnp.int32, (2 * C1, 2 * C1), 0) // C1
    j = lax.broadcasted_iota(jnp.int32, (2 * C1, 2 * C1), 1) // C1
    return jnp.where(i == j, 1.0 / C1, 0.0).astype(bf16)


def activate(pair, gain2, mean_of):
    centred = pair.astype(f32) - dot(pair, mean_of)
    squares = centred * centred
    high = squares.astype(bf16)
    low = (squares - high.astype(f32)).astype(bf16)
    spread = dot(high, mean_of) + dot(low, mean_of)
    y = centred * lax.rsqrt(spread + epsilon) * gain2
    return y / (1.0 + jnp.exp(-y))


def store_shifted(taps, row, act):
    col = lax.broadcasted_iota(jnp.int32, act.shape, 0)
    at = pl.ds(row * COLS, COLS)
    taps[0, at, :] = jnp.where(col == 0, 0.0, pltpu.roll(act, 1, 0)).astype(bf16)
    taps[1, at, :] = act.astype(bf16)
    taps[2, at, :] = jnp.where(col == COLS - 1, 0.0, pltpu.roll(act, COLS - 1, 0)).astype(bf16)


def pair_of(ref, i):
    return jnp.concatenate([ref[0, i], ref[1, i]], axis=1)


def fill_taps(taps, rows, gain_ref, batch):
    gain2 = jnp.concatenate([gain_ref[...], gain_ref[...]], axis=1)
    mean_of = averaging()
    for start in range(0, len(rows), batch):
        some = rows[start : start + batch]
        pairs = jnp.concatenate([pair_of(ref, i) for _, ref, i, _ in some], axis=0)
        acts = activate(pairs, gain2, mean_of)
        for place, (row, _, _, factor) in enumerate(some):
            act = acts[place * COLS : (place + 1) * COLS]
            store_shifted(taps, row, act if factor is None else act * factor)


SIZE = (ROWS + 1) * COLS


def conv1_taps(taps, weight, acc, base):
    for kr, out, row, count in ((1, 0, 0, ROWS), (0, 1, 0, ROWS), (2, 0, 1, ROWS - 1)):
        tile = jnp.concatenate(
            [taps[kc, row * COLS : (row + count) * COLS, :] for kc in range(3)], axis=1
        )
        part = dot(tile, weight[kr].reshape(3 * C2, C2))
        at = pl.ds(out * COLS, count * COLS)
        if kr == 1:
            rest = pl.ds(ROWS * COLS, COLS)
            acc[at, :] = base(at) + part
            acc[rest, :] = base(rest)
        else:
            acc[at, :] += part


def stack(a, b, c, d):
    return jnp.concatenate([jnp.concatenate([a, b], axis=1), jnp.concatenate([c, d], axis=1)], axis=0)


def edge_kernel(video, bottom, top, sem):
    copies = [
        pltpu.make_async_copy(video.at[:, ROWS - 1 : ROWS], bottom, sem.at[0]),
        pltpu.make_async_copy(video.at[:, 0:2], top, sem.at[1]),
    ]
    for copy in copies:
        copy.start()
    for copy in copies:
        copy.wait()


def own_kernel(
    video_h, gain_h, bias_h, conv_h, down_h, query_h, key_h, value_h, output_h, down_bias_h, attention_gain_h,
    acc, now, before, down, query, key, value_t, output, gain, down_bias, attention_gain,
    taps, video, bias, conv, value, sem,
):
    pairs = (
        (gain_h, gain), (video_h, video), (bias_h, bias), (conv_h, conv), (value_h, value), (down_h, down),
        (query_h, query), (key_h, key), (output_h, output),
        (down_bias_h, down_bias), (attention_gain_h, attention_gain),
    )
    copies = [pltpu.make_async_copy(src, dst, sem.at[i]) for i, (src, dst) in enumerate(pairs)]
    for copy in copies:
        copy.start()
    for copy in copies[:3]:
        copy.wait()
    fill_taps(taps, [(row, video, row, None) for row in range(ROWS)], gain, 4)
    copies[3].wait()
    none = jnp.zeros((C1, C1), bf16)
    for kr in range(3):
        for kc in range(3):
            w0, w1, w2 = (conv[kt, kr, kc] for kt in range(3))
            now[kr, kc] = stack(w2, w1, none, w2)
            before[kr, kc] = stack(w0, none, w1, w0)

    def base(at):
        bias2 = jnp.concatenate([bias[...], bias[...]], axis=1)
        if at.start:
            return jnp.broadcast_to(bias2, (COLS, C2))
        return jnp.concatenate([pair_of(video, i).astype(f32) for i in range(ROWS)], axis=0) + bias2

    conv1_taps(taps, now, acc, base)
    copies[4].wait()
    value_t[...] = value[...].astype(f32).T.astype(bf16)
    for copy in copies[5:]:
        copy.wait()


TAPS = [(kr, kc) for kr in range(3) for kc in range(3)]


def down_taps(half_taps, lanes):
    starts = (0, 5 * HALF, HALF)
    tiles = [half_taps[kc, starts[kr] : starts[kr] + QUERIES, lanes] for kr, kc in TAPS]
    return jnp.concatenate(tiles, axis=1)


def fill_half_taps(half_taps, wide, rows, value):
    for row in rows:
        at = pl.ds(row * COLS, COLS)
        summed = value(row).astype(bf16).astype(f32)
        wide[0, at, :] = summed[:, :C1]
        wide[1, at, :] = summed[:, C1:]
    j = lax.broadcasted_iota(jnp.int32, (HALF, C1), 0)
    for row in rows:
        place = row // 2 if row % 2 == 0 else 5 + row // 2
        for frame in range(2):
            even = wide[frame, pl.ds(row * COLS, HALF, stride=2), :]
            odd = wide[frame, pl.ds(row * COLS + 1, HALF, stride=2), :]
            after = jnp.where(j == HALF - 1, 0.0, pltpu.roll(even, HALF - 1, 0))
            lanes = pl.ds(frame * C1, C1)
            at = pl.ds(place * HALF, HALF)
            half_taps[0, at, lanes] = even.astype(bf16)
            half_taps[1, at, lanes] = odd.astype(bf16)
            half_taps[2, at, lanes] = after.astype(bf16)


def send_down(send, half_taps, down, places):
    def tile(lanes):
        columns = [
            jnp.concatenate([half_taps[kc, p * HALF : (p + 1) * HALF, lanes] for p in places[kr]], axis=0)
            for kr, kc in TAPS
        ]
        return jnp.concatenate(columns, axis=1)

    send[0] = dot(tile(slice(None)), down_weights(down, (0, 1))).astype(bf16)
    send[1] = dot(tile(slice(C1, None)), down_weights(down, (0,))).astype(bf16)


def down_weights(down, times):
    return jnp.concatenate([down[kt, kr, kc] for kr, kc in TAPS for kt in times], axis=0)


def halo_kernel(flags, acc_in, halo, gain, weight, down, acc, send, taps, wide, half_taps):
    fill_taps(taps, [(row, halo, row, flags[0]) for row in range(ROWS)], gain, 4)
    conv1_taps(taps, weight, acc, lambda at: acc_in[at, :])
    fill_half_taps(half_taps, wide, range(2, ROWS - 1), lambda row: acc[pl.ds(row * COLS, COLS), :])
    send_down(send, half_taps, down, ((1, 2), (6, 7), (2, 3)))


def sum_kernel(
    flags, acc, above, below, far_above, far_below, gain, now, before, down,
    send, half_taps, taps, wide,
):
    past = flags[0]
    edges = [(0, above, 0, flags[1]), (1, below, 0, flags[2]), (2, below, 1, flags[2])]
    far = [(3, far_above, 0, flags[1]), (4, far_below, 0, flags[2]), (5, far_below, 1, flags[2])]
    fill_taps(taps, edges + [(row, ref, i, factor * past) for row, ref, i, factor in far], gain, 3)

    def extra(kr, row, count):
        tile = jnp.concatenate(
            [
                taps[kc, (base + row) * COLS : (base + row + count) * COLS, :]
                for base in (0, 3)
                for kc in range(3)
            ],
            axis=1,
        )
        weight = jnp.concatenate([now[kr].reshape(3 * C2, C2), before[kr].reshape(3 * C2, C2)], axis=0)
        return dot(tile, weight)

    last = extra(2, 1, 2)
    extras = {0: extra(0, 0, 1), ROWS - 1: last[:COLS]}
    extras[ROWS] = last[COLS:] + extra(1, 1, 1) + pair_of(below, 0).astype(f32)
    def value(row):
        at = pl.ds(row * COLS, COLS)
        total = acc[at, :] + extras[row] if row in extras else acc[at, :]
        return total * flags[2] if row == ROWS else total

    fill_half_taps(half_taps, wide, range(ROWS + 1), value)
    send_down(send, half_taps, down, ((0, 3), (5, 8), (1, 4)))


def normalise(value, gain):
    centred = value - jnp.mean(value, axis=2, keepdims=True)
    spread = jnp.mean(centred * centred, axis=2, keepdims=True)
    return (centred * lax.rsqrt(spread + epsilon) * gain[...]).astype(bf16)


INNER = slice(HALF, 3 * HALF)


def down_kernel(flags, half_taps, down, bias, inner, gain, out, normed):
    out[0] = dot(down_taps(half_taps, slice(0, C1)), down_weights(down, (2,))) + bias[...]
    out[1] = dot(down_taps(half_taps, slice(None)), down_weights(down, (1, 2))) + bias[...]
    value = out[:, INNER, :] + inner[...].astype(f32) * flags[0]
    out[:, INNER, :] = value
    normed[...] = normalise(value, gain)


def norm_kernel(flags, part, outer, inner_normed, gain, reduced, normed):
    value = jnp.concatenate([part[:, :HALF], part[:, 3 * HALF :]], axis=1)
    value = value + outer[...].astype(f32) * flags[0]
    result = normalise(value, gain)
    for frame in range(2):
        for ref, edge, middle in (
            (reduced, value[frame], part[frame, INNER, :]),
            (normed, result[frame], inner_normed[frame]),
        ):
            ref[frame, :HALF, :] = edge[:HALF]
            ref[frame, INNER, :] = middle
            ref[frame, 3 * HALF :, :] = edge[HALF:]


def query_kernel(normed, weight, queries):
    for frame in range(2):
        queries[frame] = (dot(normed[frame], weight[...]).astype(bf16) * (C2**-0.5)).astype(bf16)


GROUPS = 4
STATE = C2 + 16


def attend(queries, before, outs, blocks, key_weight, value_weight_t, groups=range(4)):
    normed = jnp.concatenate([block[...] for block in blocks], axis=0)
    keys = dot(normed, key_weight[...]).astype(bf16)
    values = dot_t(value_weight_t[...], normed).astype(bf16)
    values = jnp.concatenate([values, jnp.ones((16, values.shape[1]), bf16)], axis=0)
    ahead = dot_t(keys, queries[groups[0]])
    for i, group in enumerate(groups):
        scores = ahead
        if i + 1 < len(groups):
            ahead = dot_t(keys, queries[groups[i + 1]])
        highest = jnp.max(scores, axis=0, keepdims=True)
        if before is not None:
            old = before[group, C2 + 8 : C2 + 9, :]
            highest = jnp.maximum(old, highest)
            rescale = jnp.exp(old - highest)
        weights = jnp.exp(scores - highest).astype(bf16)
        product = dot(values, weights)[: C2 + 8]
        if before is not None:
            product += before[group, : C2 + 8, :] * rescale
        out, place = outs(group)
        out[place, : C2 + 8, :] = product
        out[place, C2 + 8 :, :] = jnp.broadcast_to(highest, (8, C2))


def early_attend_kernel(frame, own, across, block, plus, minus, key_weight, value_weight_t, state):
    blocks = [ref.at[frame] for ref in (block, plus, minus)]
    queries = {0: own[frame], 1: across[frame]}
    attend(queries, None, lambda g: (state, g), blocks, key_weight, value_weight_t, (0, 1))


def first_attend_kernel(
    frame, own, sibling, across, both, early, block, plus, minus, key_weight, value_weight_t, queries, state
):
    for group, source in enumerate((own, sibling, across, both)):
        queries[group] = source[frame]
    state[0] = early[0]
    state[2] = early[1]
    blocks = [ref.at[frame] for ref in (block, plus, minus)]
    attend(queries, None, lambda g: (state, g), blocks, key_weight, value_weight_t, (1, 3))


def attend_kernel(frame, queries, before, plus, minus, key_weight, value_weight_t, state):
    blocks = [ref.at[frame] for ref in (plus, minus)]
    attend(queries, before, lambda g: (state, g), blocks, key_weight, value_weight_t)


def cut_kernel(plus, minus, first, second):
    first[...] = plus[0]
    second[...] = minus[1]


def last_attend_kernel(groups, *refs):
    queries, before, blocks = refs[0:2], refs[2:4], refs[4:6]
    key_weight, value_weight_t, mine, theirs = refs[6:]
    for frame in range(2):
        attend(
            queries[frame],
            before[frame],
            lambda g: (mine if g == groups[0] else theirs, frame),
            (blocks[frame],),
            key_weight,
            value_weight_t,
            groups,
        )


def split3(x):
    high = x.astype(bf16).astype(f32)
    middle = (x - high).astype(bf16).astype(f32)
    return [high, middle, x - high - middle]


def merged(mine, theirs, frame):
    top_a, top_b = mine[frame, C2 + 8 :, :], theirs[frame, C2 + 8 :, :]
    top = jnp.maximum(top_a, top_b)
    scale_a, scale_b = jnp.exp(top_a - top), jnp.exp(top_b - top)
    mass = mine[frame, C2 : C2 + 8, :] * scale_a + theirs[frame, C2 : C2 + 8, :] * scale_b
    return mass, top, scale_a, scale_b


def merge_keep_kernel(mine, theirs, state):
    for frame in range(2):
        mass, top, scale_a, scale_b = merged(mine, theirs, frame)
        state[frame, :C2, :] = mine[frame, :C2, :] * scale_a[:1] + theirs[frame, :C2, :] * scale_b[:1]
        state[frame, C2 : C2 + 8, :] = mass
        state[frame, C2 + 8 :, :] = top


def merge_send_kernel(mine, theirs, send):
    for frame in range(2):
        mass, top, scale_a, scale_b = merged(mine, theirs, frame)
        inverse = 1.0 / mass
        scale_a, scale_b = scale_a * inverse, scale_b * inverse
        total = mine[frame, :C2, :] * scale_a[:1] + theirs[frame, :C2, :] * scale_b[:1]
        send[frame, :C2, :] = total.astype(bf16)
        rows = split3(top[:1]) + split3(mass[:1]) + [jnp.zeros((10, C2), f32)]
        send[frame, C2:, :] = jnp.concatenate(rows, axis=0).astype(bf16)


def last_kernel(reduced, state, received, weight, out, held, sem):
    copies = []
    for frame in range(2):
        rows = received[frame, C2:, :].astype(f32)
        top_a, mass_a = state[frame, C2 + 8 : C2 + 9, :], state[frame, C2 : C2 + 1, :]
        top_b = rows[0:1] + rows[1:2] + rows[2:3]
        mass_b = rows[3:4] + rows[4:5] + rows[5:6]
        top = jnp.maximum(top_a, top_b)
        scale_a = jnp.exp(top_a - top)
        scale_b = jnp.exp(top_b - top) * mass_b
        inverse = 1.0 / (mass_a * scale_a + scale_b)
        attended = state[frame, :C2, :] * (scale_a * inverse)
        attended += received[frame, :C2, :].astype(f32) * (scale_b * inverse)
        mixed = lax.dot_general(
            attended.astype(bf16), weight[...], (((0,), (0,)), ((), ())), preferred_element_type=f32
        )
        held[frame] = reduced[frame] + mixed
        copies.append(pltpu.make_async_copy(held.at[frame], out.at[frame], sem.at[frame]))
        copies[frame].start()
    for copy in copies:
        copy.wait()


def body(
    video,
    norm_gain,
    conv_weight,
    conv_bias,
    down_weight,
    down_bias,
    attention_gain,
    query_weight,
    key_weight,
    value_weight,
    output_weight,
):
    space = lax.axis_size("space")
    times = lax.axis_size("tm")
    place = lax.axis_index("space")
    has = [lax.axis_index("tm") > 0, place > 0, place < space - 1]
    flags = jnp.stack(has).astype(f32)
    scalar = {0: SMEM}

    def next_frames(x):
        return lax.ppermute(x, "tm", [(i, (i + 1) % times) for i in range(times)])

    def along(x, distance):
        return lax.ppermute(x, "space", [(i, (i + distance) % space) for i in range(space)])

    def diagonal(x, distance):
        route = [
            (t * space + i, ((t + 1) % times) * space + (i + distance) % space)
            for t in range(times)
            for i in range(space)
        ]
        return lax.ppermute(x, ("tm", "space"), route)

    def swap(x, bit):
        return lax.ppermute(x, "space", [(i, i ^ bit) for i in range(space)])

    bottom, top = call(
        edge_kernel,
        [((2, 1, COLS, C1), bf16), ((2, 2, COLS, C1), bf16)],
        [video],
        [pltpu.SemaphoreType.DMA((2,))],
        {0: HBM},
        nbytes=400_000,
    )
    above = along(bottom, 1)
    below = along(top, -1)
    halo = next_frames(video)
    far_above, far_below = diagonal(bottom, 1), diagonal(top, -1)

    square = (C2, C2)
    taps = pltpu.VMEM((3, ROWS * COLS, C2), bf16)
    whole = ((SIZE, C2), f32)
    prepared = (3, 3) + square
    (
        acc, now, before, down_weight, query_weight, key_weight, value_weight, output_weight,
        gain, down_bias, attention_gain,
    ) = call(
        own_kernel,
        [whole, (prepared, bf16), (prepared, bf16), (down_weight.shape, bf16)]
        + [(square, bf16)] * 4
        + [((1, C1), f32), ((1, C2), f32), ((1, C2), f32)],
        [video, norm_gain.reshape(1, C1), conv_bias.reshape(1, C1), conv_weight, down_weight]
        + [query_weight, key_weight, value_weight, output_weight]
        + [down_bias.reshape(1, C2), attention_gain.reshape(1, C2)],
        [
            taps,
            pltpu.VMEM(video.shape, bf16),
            pltpu.VMEM((1, C1), f32),
            pltpu.VMEM(conv_weight.shape, bf16),
            pltpu.VMEM(square, bf16),
            pltpu.SemaphoreType.DMA((11,)),
        ],
        {i: HBM for i in range(11)},
        flops=2 * 9 * SIZE * 256 * 256,
        nbytes=6_000_000,
    )
    wide = pltpu.VMEM((2, SIZE, C1), f32)
    half = ((3, 9 * HALF, C2), bf16)
    some = ((2, QUERIES // 2, C2), bf16)
    acc, send_inner = call(
        halo_kernel,
        [whole, some],
        [flags, acc, halo, gain, before, down_weight],
        [taps, wide, pltpu.VMEM(*half)],
        scalar,
        flops=2 * 9 * SIZE * 256 * 256,
        nbytes=5_000_000,
    )
    received_inner = next_frames(send_inner)
    send, half_taps = call(
        sum_kernel,
        [some, half],
        [flags, acc, above, below, far_above, far_below, gain, now, before, down_weight],
        [pltpu.VMEM((3, 6 * COLS, C2), bf16), wide],
        scalar,
        flops=2 * 18 * 256 * 256 * 256,
        nbytes=5_000_000,
    )
    received = next_frames(send)
    part, inner = call(
        down_kernel,
        [((2, QUERIES, C2), f32), some],
        [flags, half_taps, down_weight, down_bias, received_inner, attention_gain],
        spaces=scalar,
        flops=2 * 18 * 256 * 256 * 256,
        nbytes=3_000_000,
    )
    pixels = ((2, QUERIES, C2), bf16)
    reduced, normed = call(
        norm_kernel,
        [((2, QUERIES, C2), f32), pixels],
        [flags, part, received, inner, attention_gain],
        spaces=scalar,
        nbytes=2_000_000,
    )
    plus, minus = [along(normed, 4)], [along(normed, -4)]
    (own,) = call(query_kernel, [pixels], [normed, query_weight], nbytes=600_000)
    plus.append(along(plus[0], 4))
    minus.append(along(minus[0], -4))
    sibling, across = swap(own, 1), swap(own, 2)
    both = swap(across, 1)
    state = [((GROUPS, STATE, C2), f32)]
    flops = 2 * QUERIES * 256 * (512 + 2 * GROUPS * QUERIES)
    carry, queries = [0, 0], [0, 0]
    weights = [key_weight, value_weight]
    early = [0, 0]
    for frame in range(2):
        (early[frame],) = call(
            lambda *refs: early_attend_kernel(frame, *refs),
            [((2, STATE, C2), f32)],
            [own, across, normed, plus[0], minus[0]] + weights,
            flops=2 * flops,
            nbytes=3_000_000,
        )
    (sent, other), early = lax.optimization_barrier(((plus[1], minus[1]), early))
    plus.append(along(sent, 4))
    minus.append(along(other, -4))
    for frame in range(2):
        queries[frame], carry[frame] = call(
            lambda *refs: first_attend_kernel(frame, *refs),
            [((GROUPS, QUERIES, C2), bf16)] + state,
            [own, sibling, across, both, early[frame], normed, plus[0], minus[0]] + weights,
            flops=2 * flops,
            nbytes=4_000_000,
        )

    def step_on(step, frame):
        (carry[frame],) = call(
            lambda *refs: attend_kernel(frame, *refs),
            state,
            [queries[frame], carry[frame], plus[step], minus[step]] + weights,
            aliases={1: 0},
            flops=2 * flops,
            nbytes=4_000_000,
        )

    step_on(1, 0)
    (plus[2], minus[2]), carry = lax.optimization_barrier(((plus[2], minus[2]), carry))
    ends = call(cut_kernel, [((QUERIES, C2), bf16)] * 2, [plus[2], minus[2]], nbytes=500_000)
    ends = [along(ends[0], 4), along(ends[1], -4)]
    step_on(1, 1)
    step_on(2, 0)
    step_on(2, 1)
    pair = ((2, STATE, C2), f32)

    def finish(groups):
        mine, theirs = call(
            lambda *refs: last_attend_kernel(groups, *refs),
            [pair, pair],
            [*queries, *carry, *ends] + weights,
            flops=flops,
            nbytes=4_000_000,
        )
        return mine, swap(theirs, 1)

    (give,) = call(
        merge_send_kernel, [((2, STATE, C2), bf16)], list(finish((2, 3))), nbytes=1_500_000
    )
    received = swap(give, 2)
    (kept,) = call(merge_keep_kernel, [pair], list(finish((0, 1))), nbytes=2_000_000)
    (encoded,) = call(
        last_kernel,
        [((2, QUERIES, C2), f32)],
        [reduced, kept, received, output_weight],
        [pltpu.VMEM((2, QUERIES, C2), f32), pltpu.SemaphoreType.DMA((2,))],
        out_space=HBM,
        nbytes=2_000_000,
    )
    return encoded.reshape(2, ROWS // 2, HALF, C2)


def solution(mesh):
    in_specs = (P("tm", "space", None, None), P(), P(), P(), P(), P(), P(), P(), P(), P(), P())
    out_specs = P("tm", "space", None, None)
    return jax.shard_map(body, mesh=mesh, in_specs=in_specs, out_specs=out_specs, check_vma=False)
```

```python
import jax
import jax.numpy as jnp
from jax import lax
from jax.experimental import pallas as pl
from jax.experimental.pallas import tpu as pltpu
from jax.sharding import PartitionSpec as P

epsilon = 1e-05
f32 = jnp.float32
bf16 = jnp.bfloat16
VMEM = pl.BlockSpec(memory_space=pltpu.VMEM)
SMEM = pl.BlockSpec(memory_space=pltpu.SMEM)
HBM = pl.BlockSpec(memory_space=pltpu.HBM)
COLS = 128
C1 = 128
C2 = 256
ROWS = 8
HALF = 64
QUERIES = 256


def call(kernel, outs, ins, scratch=(), spaces=None, aliases=None, flops=0, nbytes=0):
    spaces = spaces or {}
    ins = [
        pltpu.with_memory_space_constraint(x, pltpu.HBM) if spaces.get(i) is HBM else x
        for i, x in enumerate(ins)
    ]
    return pl.pallas_call(
        kernel,
        out_shape=[jax.ShapeDtypeStruct(s, d) for s, d in outs],
        in_specs=[spaces.get(i, VMEM) for i in range(len(ins))],
        out_specs=[VMEM] * len(outs),
        scratch_shapes=list(scratch),
        input_output_aliases=aliases or {},
        compiler_params=pltpu.CompilerParams(vmem_limit_bytes=24 * 1024 * 1024),
        cost_estimate=pl.CostEstimate(flops=flops, bytes_accessed=nbytes, transcendentals=0),
    )(*ins)


def dot(a, b):
    return jnp.dot(a, b, preferred_element_type=f32)


def dot_t(a, b):
    return lax.dot_general(a, b, (((1,), (1,)), ((), ())), preferred_element_type=f32)


def averaging():
    i = lax.broadcasted_iota(jnp.int32, (2 * C1, 2 * C1), 0) // C1
    j = lax.broadcasted_iota(jnp.int32, (2 * C1, 2 * C1), 1) // C1
    return jnp.where(i == j, 1.0 / C1, 0.0).astype(bf16)


def activate(pair, gain2, mean_of):
    centred = pair.astype(f32) - dot(pair, mean_of)
    squares = centred * centred
    high = squares.astype(bf16)
    low = (squares - high.astype(f32)).astype(bf16)
    spread = dot(high, mean_of) + dot(low, mean_of)
    y = centred * lax.rsqrt(spread + epsilon) * gain2
    return y / (1.0 + jnp.exp(-y))


def store_shifted(taps, row, act):
    col = lax.broadcasted_iota(jnp.int32, act.shape, 0)
    at = pl.ds(row * COLS, COLS)
    taps[0, at, :] = jnp.where(col == 0, 0.0, pltpu.roll(act, 1, 0)).astype(bf16)
    taps[1, at, :] = act.astype(bf16)
    taps[2, at, :] = jnp.where(col == COLS - 1, 0.0, pltpu.roll(act, COLS - 1, 0)).astype(bf16)


def pair_of(ref, i):
    return jnp.concatenate([ref[0, i], ref[1, i]], axis=1)


def fill_taps(taps, rows, gain_ref, batch):
    gain2 = jnp.concatenate([gain_ref[...], gain_ref[...]], axis=1)
    mean_of = averaging()
    for start in range(0, len(rows), batch):
        some = rows[start : start + batch]
        pairs = jnp.concatenate([pair_of(ref, i) for _, ref, i, _ in some], axis=0)
        acts = activate(pairs, gain2, mean_of)
        for place, (row, _, _, factor) in enumerate(some):
            act = acts[place * COLS : (place + 1) * COLS]
            store_shifted(taps, row, act if factor is None else act * factor)


SIZE = (ROWS + 1) * COLS


def conv1_taps(taps, weight, acc, base):
    for kr, out, row, count in ((1, 0, 0, ROWS), (0, 1, 0, ROWS), (2, 0, 1, ROWS - 1)):
        tile = jnp.concatenate(
            [taps[kc, row * COLS : (row + count) * COLS, :] for kc in range(3)], axis=1
        )
        part = dot(tile, weight[kr].reshape(3 * C2, C2))
        at = pl.ds(out * COLS, count * COLS)
        if kr == 1:
            rest = pl.ds(ROWS * COLS, COLS)
            acc[at, :] = base(at) + part
            acc[rest, :] = base(rest)
        else:
            acc[at, :] += part


def stack(a, b, c, d):
    return jnp.concatenate([jnp.concatenate([a, b], axis=1), jnp.concatenate([c, d], axis=1)], axis=0)


def edge_kernel(video, bottom, top, sem):
    copies = [
        pltpu.make_async_copy(video.at[:, ROWS - 1 : ROWS], bottom, sem.at[0]),
        pltpu.make_async_copy(video.at[:, 0:2], top, sem.at[1]),
    ]
    for copy in copies:
        copy.start()
    for copy in copies:
        copy.wait()


def own_kernel(
    video_h, gain_h, bias_h, conv_h, down_h, query_h, key_h, value_h, output_h, down_bias_h, attention_gain_h,
    acc, now, before, down, query, key, value_t, output, gain, down_bias, attention_gain,
    taps, video, bias, conv, value, sem,
):
    pairs = (
        (gain_h, gain), (video_h, video), (bias_h, bias), (conv_h, conv), (value_h, value), (down_h, down),
        (query_h, query), (key_h, key), (output_h, output),
        (down_bias_h, down_bias), (attention_gain_h, attention_gain),
    )
    copies = [pltpu.make_async_copy(src, dst, sem.at[i]) for i, (src, dst) in enumerate(pairs)]
    for copy in copies:
        copy.start()
    for copy in copies[:3]:
        copy.wait()
    fill_taps(taps, [(row, video, row, None) for row in range(ROWS)], gain, 4)
    copies[3].wait()
    none = jnp.zeros((C1, C1), bf16)
    for kr in range(3):
        for kc in range(3):
            w0, w1, w2 = (conv[kt, kr, kc] for kt in range(3))
            now[kr, kc] = stack(w2, w1, none, w2)
            before[kr, kc] = stack(w0, none, w1, w0)

    def base(at):
        bias2 = jnp.concatenate([bias[...], bias[...]], axis=1)
        if at.start:
            return jnp.broadcast_to(bias2, (COLS, C2))
        return jnp.concatenate([pair_of(video, i).astype(f32) for i in range(ROWS)], axis=0) + bias2

    conv1_taps(taps, now, acc, base)
    copies[4].wait()
    value_t[...] = value[...].astype(f32).T.astype(bf16)
    for copy in copies[5:]:
        copy.wait()


TAPS = [(kr, kc) for kr in range(3) for kc in range(3)]


def down_taps(half_taps, lanes):
    starts = (0, 5 * HALF, HALF)
    tiles = [half_taps[kc, starts[kr] : starts[kr] + QUERIES, lanes] for kr, kc in TAPS]
    return jnp.concatenate(tiles, axis=1)


def fill_half_taps(half_taps, wide, rows, value):
    for row in rows:
        at = pl.ds(row * COLS, COLS)
        summed = value(row).astype(bf16).astype(f32)
        wide[0, at, :] = summed[:, :C1]
        wide[1, at, :] = summed[:, C1:]
    j = lax.broadcasted_iota(jnp.int32, (HALF, C1), 0)
    for row in rows:
        place = row // 2 if row % 2 == 0 else 5 + row // 2
        for frame in range(2):
            even = wide[frame, pl.ds(row * COLS, HALF, stride=2), :]
            odd = wide[frame, pl.ds(row * COLS + 1, HALF, stride=2), :]
            after = jnp.where(j == HALF - 1, 0.0, pltpu.roll(even, HALF - 1, 0))
            lanes = pl.ds(frame * C1, C1)
            at = pl.ds(place * HALF, HALF)
            half_taps[0, at, lanes] = even.astype(bf16)
            half_taps[1, at, lanes] = odd.astype(bf16)
            half_taps[2, at, lanes] = after.astype(bf16)


def send_down(send, half_taps, down, places):
    def tile(lanes):
        columns = [
            jnp.concatenate([half_taps[kc, p * HALF : (p + 1) * HALF, lanes] for p in places[kr]], axis=0)
            for kr, kc in TAPS
        ]
        return jnp.concatenate(columns, axis=1)

    send[0] = dot(tile(slice(None)), down_weights(down, (0, 1))).astype(bf16)
    send[1] = dot(tile(slice(C1, None)), down_weights(down, (0,))).astype(bf16)


def down_weights(down, times):
    return jnp.concatenate([down[kt, kr, kc] for kr, kc in TAPS for kt in times], axis=0)


def halo_kernel(flags, acc_in, halo, gain, weight, down, acc, send, taps, wide, half_taps):
    fill_taps(taps, [(row, halo, row, flags[0]) for row in range(ROWS)], gain, 4)
    conv1_taps(taps, weight, acc, lambda at: acc_in[at, :])
    fill_half_taps(half_taps, wide, range(2, ROWS - 1), lambda row: acc[pl.ds(row * COLS, COLS), :])
    send_down(send, half_taps, down, ((1, 2), (6, 7), (2, 3)))


def sum_kernel(
    flags, acc, above, below, far_above, far_below, gain, now, before, down,
    send, half_taps, taps, wide,
):
    past = flags[0]
    edges = [(0, above, 0, flags[1]), (1, below, 0, flags[2]), (2, below, 1, flags[2])]
    far = [(3, far_above, 0, flags[1]), (4, far_below, 0, flags[2]), (5, far_below, 1, flags[2])]
    fill_taps(taps, edges + [(row, ref, i, factor * past) for row, ref, i, factor in far], gain, 6)

    def extra(kr, row, count):
        tile = jnp.concatenate(
            [
                taps[kc, (base + row) * COLS : (base + row + count) * COLS, :]
                for base in (0, 3)
                for kc in range(3)
            ],
            axis=1,
        )
        weight = jnp.concatenate([now[kr].reshape(3 * C2, C2), before[kr].reshape(3 * C2, C2)], axis=0)
        return dot(tile, weight)

    last = extra(2, 1, 2)
    extras = {0: extra(0, 0, 1), ROWS - 1: last[:COLS]}
    extras[ROWS] = last[COLS:] + extra(1, 1, 1) + pair_of(below, 0).astype(f32)
    def value(row):
        at = pl.ds(row * COLS, COLS)
        total = acc[at, :] + extras[row] if row in extras else acc[at, :]
        return total * flags[2] if row == ROWS else total

    fill_half_taps(half_taps, wide, range(ROWS + 1), value)
    send_down(send, half_taps, down, ((0, 3), (5, 8), (1, 4)))


def down_kernel(flags, half_taps, down, bias, inner, out):
    out[0] = dot(down_taps(half_taps, slice(0, C1)), down_weights(down, (2,))) + bias[...]
    out[1] = dot(down_taps(half_taps, slice(None)), down_weights(down, (1, 2))) + bias[...]
    at = pl.ds(HALF, 2 * HALF)
    out[:, at, :] += inner[...].astype(f32) * flags[0]


def norm_kernel(flags, part, outer, gain, query_weight, reduced, normed, queries):
    more = outer[...].astype(f32) * flags[0]
    pieces = [part[:, :HALF] + more[:, :HALF], part[:, HALF : 3 * HALF], part[:, 3 * HALF :] + more[:, HALF:]]
    value = jnp.concatenate(pieces, axis=1)
    reduced[...] = value
    centred = value - jnp.mean(value, axis=2, keepdims=True)
    spread = jnp.mean(centred * centred, axis=2, keepdims=True)
    result = (centred * lax.rsqrt(spread + epsilon) * gain[...]).astype(bf16)
    normed[...] = result
    for frame in range(2):
        queries[frame] = (dot(result[frame], query_weight[...]).astype(bf16) * (C2**-0.5)).astype(bf16)


GROUPS = 4
STATE = C2 + 16


def attend(queries, before, outs, blocks, key_weight, value_weight_t, groups=range(4)):
    normed = jnp.concatenate([block[...] for block in blocks], axis=0)
    keys = dot(normed, key_weight[...]).astype(bf16)
    values = dot_t(value_weight_t[...], normed).astype(bf16)
    values = jnp.concatenate([values, jnp.ones((16, values.shape[1]), bf16)], axis=0)
    ahead = dot_t(keys, queries[groups[0]])
    for i, group in enumerate(groups):
        scores = ahead
        if i + 1 < len(groups):
            ahead = dot_t(keys, queries[groups[i + 1]])
        highest = jnp.max(scores, axis=0, keepdims=True)
        if before is not None:
            old = before[group, C2 + 8 : C2 + 9, :]
            highest = jnp.maximum(old, highest)
            rescale = jnp.exp(old - highest)
        weights = jnp.exp(scores - highest).astype(bf16)
        product = dot(values, weights)[: C2 + 8]
        if before is not None:
            product += before[group, : C2 + 8, :] * rescale
        out, place = outs(group)
        out[place, : C2 + 8, :] = product
        out[place, C2 + 8 :, :] = jnp.broadcast_to(highest, (8, C2))


def early_attend_kernel(frame, own, across, block, plus, minus, key_weight, value_weight_t, state):
    blocks = [ref.at[frame] for ref in (block, plus, minus)]
    queries = {0: own[frame], 1: across[frame]}
    attend(queries, None, lambda g: (state, g), blocks, key_weight, value_weight_t, (0, 1))


def first_attend_kernel(
    frame, own, sibling, across, both, early, block, plus, minus, key_weight, value_weight_t, queries, state
):
    for group, source in enumerate((own, sibling, across, both)):
        queries[group] = source[frame]
    state[0] = early[0]
    state[2] = early[1]
    blocks = [ref.at[frame] for ref in (block, plus, minus)]
    attend(queries, None, lambda g: (state, g), blocks, key_weight, value_weight_t, (1, 3))


def attend_kernel(frame, queries, before, plus, minus, key_weight, value_weight_t, state):
    blocks = [ref.at[frame] for ref in (plus, minus)]
    attend(queries, before, lambda g: (state, g), blocks, key_weight, value_weight_t)


def cut_kernel(plus, minus, first, second):
    first[...] = plus[0]
    second[...] = minus[1]


def last_attend_kernel(groups, *refs):
    queries, before, blocks = refs[0:2], refs[2:4], refs[4:6]
    key_weight, value_weight_t, mine, theirs = refs[6:]
    for frame in range(2):
        attend(
            queries[frame],
            before[frame],
            lambda g: (mine if g == groups[0] else theirs, frame),
            (blocks[frame],),
            key_weight,
            value_weight_t,
            groups,
        )


def split3(x):
    high = x.astype(bf16).astype(f32)
    middle = (x - high).astype(bf16).astype(f32)
    return [high, middle, x - high - middle]


def merged(mine, theirs, frame):
    top_a, top_b = mine[frame, C2 + 8 :, :], theirs[frame, C2 + 8 :, :]
    top = jnp.maximum(top_a, top_b)
    scale_a, scale_b = jnp.exp(top_a - top), jnp.exp(top_b - top)
    mass = mine[frame, C2 : C2 + 8, :] * scale_a + theirs[frame, C2 : C2 + 8, :] * scale_b
    return mass, top, scale_a, scale_b


def merge_keep_kernel(mine, theirs, state):
    for frame in range(2):
        mass, top, scale_a, scale_b = merged(mine, theirs, frame)
        state[frame, :C2, :] = mine[frame, :C2, :] * scale_a[:1] + theirs[frame, :C2, :] * scale_b[:1]
        state[frame, C2 : C2 + 8, :] = mass
        state[frame, C2 + 8 :, :] = top


def merge_send_kernel(mine, theirs, send):
    for frame in range(2):
        mass, top, scale_a, scale_b = merged(mine, theirs, frame)
        inverse = 1.0 / mass
        scale_a, scale_b = scale_a * inverse, scale_b * inverse
        total = mine[frame, :C2, :] * scale_a[:1] + theirs[frame, :C2, :] * scale_b[:1]
        send[frame, :C2, :] = total.astype(bf16)
        rows = split3(top[:1]) + split3(mass[:1]) + [jnp.zeros((10, C2), f32)]
        send[frame, C2:, :] = jnp.concatenate(rows, axis=0).astype(bf16)


def last_kernel(reduced, state, received, weight, out):
    for frame in range(2):
        rows = received[frame, C2:, :].astype(f32)
        top_a, mass_a = state[frame, C2 + 8 : C2 + 9, :], state[frame, C2 : C2 + 1, :]
        top_b = rows[0:1] + rows[1:2] + rows[2:3]
        mass_b = rows[3:4] + rows[4:5] + rows[5:6]
        top = jnp.maximum(top_a, top_b)
        scale_a = jnp.exp(top_a - top)
        scale_b = jnp.exp(top_b - top) * mass_b
        inverse = 1.0 / (mass_a * scale_a + scale_b)
        attended = state[frame, :C2, :] * (scale_a * inverse)
        attended += received[frame, :C2, :].astype(f32) * (scale_b * inverse)
        mixed = lax.dot_general(
            attended.astype(bf16), weight[...], (((0,), (0,)), ((), ())), preferred_element_type=f32
        )
        out[frame] = reduced[frame] + mixed


def body(
    video,
    norm_gain,
    conv_weight,
    conv_bias,
    down_weight,
    down_bias,
    attention_gain,
    query_weight,
    key_weight,
    value_weight,
    output_weight,
):
    space = lax.axis_size("space")
    times = lax.axis_size("tm")
    place = lax.axis_index("space")
    has = [lax.axis_index("tm") > 0, place > 0, place < space - 1]
    flags = jnp.stack(has).astype(f32)
    scalar = {0: SMEM}

    def next_frames(x):
        return lax.ppermute(x, "tm", [(i, (i + 1) % times) for i in range(times)])

    def along(x, distance):
        return lax.ppermute(x, "space", [(i, (i + distance) % space) for i in range(space)])

    def diagonal(x, distance):
        route = [
            (t * space + i, ((t + 1) % times) * space + (i + distance) % space)
            for t in range(times)
            for i in range(space)
        ]
        return lax.ppermute(x, ("tm", "space"), route)

    def swap(x, bit):
        return lax.ppermute(x, "space", [(i, i ^ bit) for i in range(space)])

    bottom, top = call(
        edge_kernel,
        [((2, 1, COLS, C1), bf16), ((2, 2, COLS, C1), bf16)],
        [video],
        [pltpu.SemaphoreType.DMA((2,))],
        {0: HBM},
        nbytes=400_000,
    )
    above = along(bottom, 1)
    below = along(top, -1)
    halo = next_frames(video)
    far_above, far_below = diagonal(bottom, 1), diagonal(top, -1)

    square = (C2, C2)
    taps = pltpu.VMEM((3, ROWS * COLS, C2), bf16)
    whole = ((SIZE, C2), f32)
    prepared = (3, 3) + square
    (
        acc, now, before, down_weight, query_weight, key_weight, value_weight, output_weight,
        gain, down_bias, attention_gain,
    ) = call(
        own_kernel,
        [whole, (prepared, bf16), (prepared, bf16), (down_weight.shape, bf16)]
        + [(square, bf16)] * 4
        + [((1, C1), f32), ((1, C2), f32), ((1, C2), f32)],
        [video, norm_gain.reshape(1, C1), conv_bias.reshape(1, C1), conv_weight, down_weight]
        + [query_weight, key_weight, value_weight, output_weight]
        + [down_bias.reshape(1, C2), attention_gain.reshape(1, C2)],
        [
            taps,
            pltpu.VMEM(video.shape, bf16),
            pltpu.VMEM((1, C1), f32),
            pltpu.VMEM(conv_weight.shape, bf16),
            pltpu.VMEM(square, bf16),
            pltpu.SemaphoreType.DMA((11,)),
        ],
        {i: HBM for i in range(11)},
        flops=2 * 9 * SIZE * 256 * 256,
        nbytes=6_000_000,
    )
    wide = pltpu.VMEM((2, SIZE, C1), f32)
    half = ((3, 9 * HALF, C2), bf16)
    some = ((2, QUERIES // 2, C2), bf16)
    acc, send_inner = call(
        halo_kernel,
        [whole, some],
        [flags, acc, halo, gain, before, down_weight],
        [taps, wide, pltpu.VMEM(*half)],
        scalar,
        flops=2 * 9 * SIZE * 256 * 256,
        nbytes=5_000_000,
    )
    received_inner = next_frames(send_inner)
    send, half_taps = call(
        sum_kernel,
        [some, half],
        [flags, acc, above, below, far_above, far_below, gain, now, before, down_weight],
        [pltpu.VMEM((3, 6 * COLS, C2), bf16), wide],
        scalar,
        flops=2 * 18 * 256 * 256 * 256,
        nbytes=5_000_000,
    )
    received = next_frames(send)
    (part,) = call(
        down_kernel,
        [((2, QUERIES, C2), f32)],
        [flags, half_taps, down_weight, down_bias, received_inner],
        spaces=scalar,
        flops=2 * 18 * 256 * 256 * 256,
        nbytes=3_000_000,
    )
    pixels = ((2, QUERIES, C2), bf16)
    reduced, normed, own = call(
        norm_kernel,
        [((2, QUERIES, C2), f32), pixels, pixels],
        [flags, part, received, attention_gain, query_weight],
        spaces=scalar,
        nbytes=2_000_000,
    )
    plus, minus = [along(normed, 4)], [along(normed, -4)]
    plus.append(along(plus[0], 4))
    minus.append(along(minus[0], -4))
    sibling, across = swap(own, 1), swap(own, 2)
    both = swap(across, 1)
    state = [((GROUPS, STATE, C2), f32)]
    flops = 2 * QUERIES * 256 * (512 + 2 * GROUPS * QUERIES)
    carry, queries = [0, 0], [0, 0]
    weights = [key_weight, value_weight]
    early = [0, 0]
    for frame in range(2):
        (early[frame],) = call(
            lambda *refs: early_attend_kernel(frame, *refs),
            [((2, STATE, C2), f32)],
            [own, across, normed, plus[0], minus[0]] + weights,
            flops=2 * flops,
            nbytes=3_000_000,
        )
    (sent, other), early = lax.optimization_barrier(((plus[1], minus[1]), early))
    plus.append(along(sent, 4))
    minus.append(along(other, -4))
    for frame in range(2):
        queries[frame], carry[frame] = call(
            lambda *refs: first_attend_kernel(frame, *refs),
            [((GROUPS, QUERIES, C2), bf16)] + state,
            [own, sibling, across, both, early[frame], normed, plus[0], minus[0]] + weights,
            flops=2 * flops,
            nbytes=4_000_000,
        )

    def step_on(step, frame):
        (carry[frame],) = call(
            lambda *refs: attend_kernel(frame, *refs),
            state,
            [queries[frame], carry[frame], plus[step], minus[step]] + weights,
            aliases={1: 0},
            flops=2 * flops,
            nbytes=4_000_000,
        )

    step_on(1, 0)
    (plus[2], minus[2]), carry = lax.optimization_barrier(((plus[2], minus[2]), carry))
    ends = call(cut_kernel, [((QUERIES, C2), bf16)] * 2, [plus[2], minus[2]], nbytes=500_000)
    ends = [along(ends[0], 4), along(ends[1], -4)]
    step_on(1, 1)
    step_on(2, 0)
    step_on(2, 1)
    pair = ((2, STATE, C2), f32)

    def finish(groups):
        mine, theirs = call(
            lambda *refs: last_attend_kernel(groups, *refs),
            [pair, pair],
            [*queries, *carry, *ends] + weights,
            flops=flops,
            nbytes=4_000_000,
        )
        return mine, swap(theirs, 1)

    (give,) = call(
        merge_send_kernel, [((2, STATE, C2), bf16)], list(finish((2, 3))), nbytes=1_500_000
    )
    received = swap(give, 2)
    (kept,) = call(merge_keep_kernel, [pair], list(finish((0, 1))), nbytes=2_000_000)
    (encoded,) = call(
        last_kernel,
        [((2, QUERIES, C2), f32)],
        [reduced, kept, received, output_weight],
        nbytes=2_000_000,
    )
    return encoded.reshape(2, ROWS // 2, HALF, C2)


def solution(mesh):
    in_specs = (P("tm", "space", None, None), P(), P(), P(), P(), P(), P(), P(), P(), P(), P())
    out_specs = P("tm", "space", None, None)
    return jax.shard_map(body, mesh=mesh, in_specs=in_specs, out_specs=out_specs, check_vma=False)
```
